256 devices in a mesh: dp: 8 (over y, z_hi), row: 4 (over x), col: 8 (over z_lo, core).
Axes of the slice: x: 4, y: 4, z: 8 (z_hi: 2, z_lo: 4; z = z_hi * 4 + z_lo), core: 2. Of those that a mesh axis runs over, the one named last changes fastest.
Arguments:
- tokens: bfloat16 [6144, 8192], P('dp', ('row', 'col')), may hold values from -6 to 6
- gate_weight: bfloat16 [8192, 14336], P(('row', 'dp'), 'col'), may hold values from -0.0625 to 0.0625
- up_weight: bfloat16 [8192, 14336], P(('row', 'dp'), 'col'), may hold values from -0.0625 to 0.0625
Outputs:
- hidden: bfloat16 [6144, 14336], P(('dp', 'row'), 'col')
The draws below stay inside these ranges and needn't reach their ends.
All inputs are finite; a program needn't handle non-finite values.
Results may differ from the reference program's by a relative error of at most 0.0015.
Values may be sent and summed in bfloat16 or wider, within the bound.
No kernel may reach another device: no remote copies, remote signals or barrier semaphores. Data moves between devices by JAX's collectives and lax.ppermute only.
A program may use at most 64 MiB of HBM per device.

```python
import jax
import jax.numpy as jnp

D = 8192
FF = 14336
TOKENS = 6144


def shard_levels(stream_key, shape, shards, least, high):
    def one(axis_at, shards_of):
        heights = jax.random.uniform(jax.random.fold_in(jax.random.fold_in(stream_key, 6), axis_at), (shards_of,), jnp.float32, least / len(shards), high / len(shards))
        return jnp.repeat(jnp.exp(heights), shape[axis_at] // shards_of).reshape((-1,) + (1,) * (len(shape) - axis_at - 1))

    loudness = one(*shards[0])
    for cut in shards[1:]:
        loudness = loudness * one(*cut)
    return loudness


def scatter_about(rng, extent, spread, reach, split=(), held_as=jnp.bfloat16):
    factor_of = shard_levels(rng, extent, split, -0.22, 0.18) if split else 1.0
    values = jax.random.normal(rng, extent, jnp.float32) * spread * factor_of
    return jnp.minimum(jnp.maximum(values, -reach), reach).astype(held_as)


def setup_inputs(seed: int = 0) -> dict:
    streams_of = jax.random.split(jax.random.key(seed), 4)
    tokens = scatter_about(streams_of[0], (TOKENS, D), 1.0, 6.0, ((0, 8), (1, 32)))
    gate_weight = scatter_about(streams_of[1], (D, FF), D ** -0.5, 0.0625, ((0, 32), (1, 8)))
    up_weight = scatter_about(streams_of[2], (D, FF), D ** -0.5, 0.0625, ((0, 32), (1, 8)))
    return {"tokens": tokens, "gate_weight": gate_weight, "up_weight": up_weight}


def reference(tokens, gate_weight, up_weight):
    gate = jnp.dot(tokens, gate_weight, preferred_element_type=jnp.float32)
    up = jnp.dot(tokens, up_weight, preferred_element_type=jnp.float32)
    return (jax.nn.silu(gate) * up).astype(jnp.bfloat16)
```

```python
import functools

import jax
import jax.numpy as jnp
from jax import lax
from jax.experimental import pallas as pl
from jax.experimental.pallas import tpu as pltpu
from jax.sharding import PartitionSpec as P

AXES = ("dp", "row", "col")
NX, NY, NZ, NC = 4, 4, 8, 2
CHUNKS = (256, 256, 256, 128)


def device_index(x, y, z, c):
    return ((y * 2 + z // 4) * NX + x) * 8 + (z % 4) * 2 + c


def move(value, target):
    pairs = []
    for x in range(NX):
        for y in range(NY):
            for z in range(NZ):
                for c in range(NC):
                    tx, ty, tz, tc = target(x, y, z, c)
                    pairs.append((device_index(x, y, z, c), device_index(tx % NX, ty % NY, tz % NZ, tc)))
    return lax.ppermute(value, AXES, pairs)


def multiply_kernel(first, last, rows, place, *refs):
    tokens, refs = refs[:16], refs[16:]
    weights, refs = refs[:4], refs[4:]
    if not first:
        incoming, refs = refs[0], refs[1:]
    outs, (lhs, rhs, lhs_sem, rhs_sem) = refs[:-4], refs[-4:]
    y, zh, zl, c, share = (place[i] for i in range(5))
    copies = []
    for d in range(4):
        at = lax.rem(y + d, 4)
        for f in range(2):
            k = at * 2 + (zh + f) % 2
            copies.append(pltpu.make_async_copy(weights[d].at[f], rhs.at[pl.ds(pl.multiple_of(k * 256, 256), 256)], rhs_sem.at[d * 2 + f]))
    for d in range(8):
        z = lax.rem(zh * 4 + zl + d, 8)
        block = lax.rem(z // 4 + zh, 2)
        for e in range(2):
            k = lax.rem(z, 4) * 2 + lax.rem(c + e, 2)
            copies.append(
                pltpu.make_async_copy(
                    tokens[d * 2 + e].at[pl.ds(pl.multiple_of(share * rows, rows), rows)],
                    lhs.at[block, :, pl.ds(pl.multiple_of(k * 256, 256), 256)],
                    lhs_sem.at[d * 2 + e],
                )
            )
    for copy in copies:
        copy.start()
    for copy in copies:
        copy.wait()
    width = rhs.shape[1] // 2
    left = lhs[...].reshape(2 * rows, lhs.shape[2])

    def part(lo, size):
        out = jnp.dot(left, rhs[:, lo : lo + size], preferred_element_type=jnp.float32)
        return out if first else incoming[:, lo : lo + size] + out

    if last:
        keep, send = outs
        for lo in range(0, width, 128):
            gate, up = part(lo, 128), part(width + lo, 128)
            hidden = (jax.nn.silu(gate) * up).astype(jnp.bfloat16)
            keep[:, lo : lo + 128] = hidden[:rows]
            send[:, lo : lo + 128] = hidden[rows:]
    else:
        for lo in range(0, 2 * width, 256):
            outs[0][:, lo : lo + 256] = part(lo, 256)


def multiply(place, tokens, weights, incoming, last):
    rows = tokens[0].shape[0] // NX
    depth, wide = 8 * 256, weights[0].shape[2]
    operands = [place, *tokens, *weights]
    specs = [pl.BlockSpec(memory_space=pltpu.SMEM)] + [pl.BlockSpec(memory_space=pl.ANY)] * 20
    if incoming is not None:
        operands.append(incoming)
        specs.append(pl.BlockSpec(memory_space=pltpu.VMEM))
    if last:
        shape = [jax.ShapeDtypeStruct((rows, wide // 2), jnp.bfloat16)] * 2
    else:
        shape = [jax.ShapeDtypeStruct((2 * rows, wide), jnp.float32)]
    return pl.pallas_call(
        functools.partial(multiply_kernel, incoming is None, last, rows),
        out_shape=shape,
        in_specs=specs,
        out_specs=[pl.BlockSpec(memory_space=pltpu.VMEM)] * len(shape),
        scratch_shapes=[
            pltpu.VMEM((2, rows, depth), jnp.bfloat16),
            pltpu.VMEM((depth, wide), jnp.bfloat16),
            pltpu.SemaphoreType.DMA((16,)),
            pltpu.SemaphoreType.DMA((8,)),
        ],
        compiler_params=pltpu.CompilerParams(vmem_limit_bytes=24 << 20),
        cost_estimate=pl.CostEstimate(flops=2 * 2 * rows * depth * wide, bytes_accessed=6 << 20, transcendentals=0),
    )(*operands)


def per_device(tokens, gate_weight, up_weight):
    dp, x, col = (lax.axis_index(a) for a in AXES)
    y, zh, zl, c = dp // 2, dp % 2, col // 2, col % 2
    half = gate_weight.shape[1] // 2

    mine, theirs, lo = [], [], 0
    for width in CHUNKS:
        low = jnp.concatenate([w[:, lo : lo + width] for w in (gate_weight, up_weight)], 1)
        high = jnp.concatenate([w[:, half + lo : half + lo + width] for w in (gate_weight, up_weight)], 1)
        mine.append(jnp.where(zh == 0, low, high))
        theirs.append(jnp.where(zh == 0, high, low))
        lo += width

    pieces = {0: tokens}
    ahead = behind = tokens
    for step in range(1, 4):
        ahead = move(ahead, lambda x, y, z, c: (x, y, z + 1, c))
        behind = move(behind, lambda x, y, z, c: (x, y, z - 1, c))
        pieces[8 - step], pieces[step] = ahead, behind
    pieces[4] = move(jnp.where(c == 0, ahead, behind), lambda x, y, z, c: (x, y, z + 1 - 2 * c, c))
    panel = []
    for d in range(8):
        panel += [pieces[d], move(pieces[d], lambda x, y, z, c: (x, y, z, 1 - c))]

    own, other = [], []
    for i in range(len(CHUNKS)):
        pair = jnp.stack([mine[i], move(theirs[i], lambda x, y, z, c: (x, y, z + 4, c))])
        weights = [pair] + [move(pair, lambda x, y, z, c, d=d: (x, y - d, z, c)) for d in range(1, 4)]
        total = None
        for r in (1, 2, 3, 0):
            share = jnp.where(c == 0, x + 4 - r, x + r) % NX
            place = jnp.stack([y, zh, zl, c, share]).astype(jnp.int32)
            out = multiply(place, panel, weights, total, r == 0)
            if r:
                total = move(out[0], lambda x, y, z, c: (x + 1 - 2 * c, y, z, c))
        own.append(out[0])
        other.append(move(out[1], lambda x, y, z, c: (x, y, z + 4, c)))
    own, other = jnp.concatenate(own, 1), jnp.concatenate(other, 1)
    return jnp.where(zh == 0, jnp.concatenate([own, other], 1), jnp.concatenate([other, own], 1))


def solution(mesh):
    return jax.shard_map(
        per_device,
        mesh=mesh,
        in_specs=(P("dp", ("row", "col")), P(("row", "dp"), "col"), P(("row", "dp"), "col")),
        out_specs=P(("dp", "row"), "col"),
        check_vma=False,
    )
```

```python
import jax
import jax.numpy as jnp
import numpy as np
from jax import lax
from jax.experimental import pallas as pl
from jax.experimental.pallas import tpu as pltpu
from jax.sharding import Mesh
from jax.sharding import PartitionSpec as P

NX, NY, NZ, NC = 4, 4, 8, 2
AXES = ("y", "zh", "x", "zl", "c")
PARTS = 2
TILE = 128
SPLITS = (512, 384)


def device_index(x, y, z, c):
    return ((y * 2 + z // 4) * NX + x) * 8 + (z % 4) * 2 + c


def side(x, c):
    return 1 - 2 * ((x + c) % 2)


def move(value, target):
    pairs = []
    for x in range(NX):
        for y in range(NY):
            for z in range(NZ):
                for c in range(NC):
                    tx, ty, tz, tc = target(x, y, z, c)
                    pairs.append((device_index(x, y, z, c), device_index(tx % NX, ty % NY, tz % NZ, tc)))
    return lax.ppermute(value, AXES, pairs)


def to_partner(x, y, z, c):
    return x + side(x, c), y, z, c


def to_antipode(x, y, z, c):
    return x, y, z + 4, c


def to_both(x, y, z, c):
    return x + side(x, c), y, z + 4, c


def to_summer(x, y, z, c):
    return x - side(x, c), y, z, c


def product_kernel(place, own, partner, *refs):
    weights, (sent, kept, lhs, rhs, lhs_sem, rhs_sem) = refs[:8], refs[8:]
    y, zh = place[0], place[1]
    rows = lhs.shape[2]
    loads = []
    for d in range(4):
        at = lax.rem(y + d, 4) * 2
        for u in range(2):
            for f in range(2):
                k = u * 8 + at + lax.rem(zh + f, 2)
                lo = 0
                for n, width in enumerate(SPLITS):
                    loads.append(
                        pltpu.make_async_copy(
                            weights[n * 4 + d].at[f * 2 + u],
                            rhs.at[pl.ds(pl.multiple_of(k * 256, 256), 256), lo : lo + width],
                            rhs_sem.at[len(loads)],
                        )
                    )
                    lo += width
    shares = [[], []]
    for group in range(2):
        for i in range(2):
            position = group * 2 + i
            for u, source in enumerate((own, partner)):
                for k in range(8):
                    shares[group].append(
                        pltpu.make_async_copy(
                            source.at[:, k, place[2 + position]],
                            lhs.at[position, :, :, (u * 8 + k) * 256 : (u * 8 + k + 1) * 256],
                            lhs_sem.at[group * 32 + len(shares[group])],
                        )
                    )
    for copy in loads + shares[0] + shares[1]:
        copy.start()
    for copy in loads:
        copy.wait()
    for group, out in ((0, sent), (1, kept)):
        for copy in shares[group]:
            copy.wait()
        left = lhs[group * 2 : group * 2 + 2].reshape(4 * rows, lhs.shape[3])
        for lo in range(0, rhs.shape[1], 256):
            hi = min(lo + 256, rhs.shape[1])
            out[:, lo:hi] = jnp.dot(left, rhs[:, lo:hi], preferred_element_type=jnp.float32)


def product(place, own, partner, weights):
    rows, wide, depth = own.shape[3], sum(SPLITS), 4096
    hbm, vmem = pl.BlockSpec(memory_space=pltpu.HBM), pl.BlockSpec(memory_space=pltpu.VMEM)
    return pl.pallas_call(
        product_kernel,
        out_shape=[jax.ShapeDtypeStruct((4 * rows, wide), jnp.float32)] * 2,
        in_specs=[pl.BlockSpec(memory_space=pltpu.SMEM)] + [hbm] * 10,
        out_specs=[vmem] * 2,
        scratch_shapes=[
            pltpu.VMEM((4, 2, rows, depth), jnp.bfloat16),
            pltpu.VMEM((depth, wide), jnp.bfloat16),
            pltpu.SemaphoreType.DMA((64,)),
            pltpu.SemaphoreType.DMA((32,)),
        ],
        compiler_params=pltpu.CompilerParams(vmem_limit_bytes=32 << 20),
        cost_estimate=pl.CostEstimate(flops=16 * rows * depth * wide, bytes_accessed=20 << 20, transcendentals=0),
    )(place, own, partner, *weights)


def gated_kernel(place, kept, received, *outs):
    zh = place[1]
    rows = outs[0].shape[0]
    for n, out in enumerate(outs):
        at = pl.multiple_of((n // 2 * 2 + lax.rem(zh + n, 2)) * rows, rows)
        total = kept[pl.ds(at, rows), :] + received[pl.ds(at, rows), :]
        for t in range(3):
            gate, up = total[:, 2 * t * TILE : (2 * t + 1) * TILE], total[:, (2 * t + 1) * TILE : (2 * t + 2) * TILE]
            out[:, t * TILE : (t + 1) * TILE] = (jax.nn.silu(gate) * up).astype(jnp.bfloat16)
        last = total[:, 6 * TILE :]
        up = pltpu.roll(last, TILE // 2, 1)
        out[:, 3 * TILE :] = (jax.nn.silu(last) * up).astype(jnp.bfloat16)[:, : TILE // 2]


def gated(place, kept, received):
    rows, wide = kept.shape
    vmem = pl.BlockSpec(memory_space=pltpu.VMEM)
    return pl.pallas_call(
        gated_kernel,
        out_shape=[jax.ShapeDtypeStruct((rows // 4, wide // 2), jnp.bfloat16)] * 4,
        in_specs=[pl.BlockSpec(memory_space=pltpu.SMEM), vmem, vmem],
        out_specs=[vmem] * 4,
        compiler_params=pltpu.CompilerParams(vmem_limit_bytes=16 << 20),
        cost_estimate=pl.CostEstimate(flops=8 * rows * wide, bytes_accessed=4 << 20, transcendentals=rows * wide // 2),
    )(place, kept, received)


def column_block(gate, up, zh, q):
    base = zh * 896
    first = base + q * 512
    tiles = []
    for t in range(3):
        cut = slice(first + t * TILE, first + (t + 1) * TILE)
        tiles += [gate[:, cut], up[:, cut]]
    cut = slice(base + 384 + q * 64, base + 448 + q * 64)
    a = jnp.concatenate(tiles[:4], 1)
    b = jnp.concatenate([*tiles[4:], gate[:, cut], up[:, cut]], 1)
    return a, b


def per_device(tokens, gate_weight, up_weight):
    y, zh, x, zl, c = (lax.axis_index(a) for a in AXES)
    ahead = side(x, c)
    partner, summer = (x + ahead + 4) % 4, (x - ahead + 4) % 4
    over = (summer - ahead + 4) % 4
    q = ((x + 1 - c) // 2) % 2
    place = jnp.stack([y, zh, summer, over, x, partner]).astype(jnp.int32)
    rows = tokens.shape[0] // NX // PARTS

    split = tokens.reshape(NX, PARTS, rows, 256)
    own, shared = [], []
    for h in range(PARTS):
        panel = lax.all_gather(split[:, h].reshape(NX * rows, 256), ("zh", "zl", "c"), axis=0)
        own.append(panel.reshape(2, 8, NX, rows, 256))
    for h in range(PARTS):
        shared.append(move(own[h], to_partner))

    weights = []
    blocks = [[column_block(gate_weight, up_weight, a, b) for b in range(2)] for a in range(2)]
    for n in range(len(SPLITS)):
        keep = [jnp.where(q == 0, blocks[a][0][n], blocks[a][1][n]) for a in range(2)]
        give = [jnp.where(q == 0, blocks[a][1][n], blocks[a][0][n]) for a in range(2)]
        got = move(jnp.stack(give), to_partner)
        mine = [jnp.where(zh == 0, keep[0], keep[1]), jnp.where(zh == 0, got[0], got[1])]
        away = jnp.stack([jnp.where(zh == 0, keep[1], keep[0]), jnp.where(zh == 0, got[1], got[0])])
        four = jnp.concatenate([jnp.stack(mine), move(away, to_antipode)])
        weights += [four] + [move(four, lambda x, y, z, c, d=d: (x, y - d, z, c)) for d in range(1, 4)]

    lines = []
    for h in range(PARTS):
        sent, kept = product(place, own[h], shared[h], weights)
        parts = gated(place, kept, move(sent, to_summer))
        parts = [parts[0]] + [move(p, t) for p, t in zip(parts[1:], (to_antipode, to_partner, to_both))]
        halves = []
        for a in range(2):
            low = jnp.where(q == 0, parts[a], parts[2 + a])
            high = jnp.where(q == 0, parts[2 + a], parts[a])
            halves.append(jnp.concatenate([low, high[:, 384:], high[:, :384]], 1))
        lines.append(jnp.where(zh == 0, jnp.concatenate(halves, 1), jnp.concatenate(halves[::-1], 1)))
    return jnp.concatenate(lines, 0)


def solution(mesh):
    fine = Mesh(np.array(mesh.devices).reshape(NY, 2, NX, NZ // 2, NC), AXES)
    rows, cols = ("y", "zh"), ("zl", "c")
    return jax.shard_map(
        per_device,
        mesh=fine,
        in_specs=(P(rows, ("x", *cols)), P(("x", *rows), cols), P(("x", *rows), cols)),
        out_specs=P((*rows, "x"), cols),
        check_vma=False,
    )
```

```python
import functools

import jax
import jax.numpy as jnp
import numpy as np
from jax import lax
from jax.experimental import pallas as pl
from jax.experimental.pallas import tpu as pltpu
from jax.sharding import Mesh
from jax.sharding import PartitionSpec as P

NX, NY, NZ, NC = 4, 4, 8, 2
AXES = ("y", "zh", "x", "zl", "c")
PARTS = 2
TILE = 128


def device_index(x, y, z, c):
    return ((y * 2 + z // 4) * NX + x) * 8 + (z % 4) * 2 + c


def side(x, c):
    return 1 - 2 * ((x + c) % 2)


def move(value, target):
    pairs = []
    for x in range(NX):
        for y in range(NY):
            for z in range(NZ):
                for c in range(NC):
                    tx, ty, tz, tc = target(x, y, z, c)
                    pairs.append((device_index(x, y, z, c), device_index(tx % NX, ty % NY, tz % NZ, tc)))
    return lax.ppermute(value, AXES, pairs)


def to_partner(x, y, z, c):
    return x + side(x, c), y, z, c


def to_crossed(x, y, z, c):
    return x + side(x, 1 - c), y, z, 1 - c


def to_antipode(x, y, z, c):
    return x, y, z + 4, c


def to_both(x, y, z, c):
    return x + side(x, c), y, z + 4, c


def to_summer(x, y, z, c):
    return x - side(x, c), y, z, c


def product_kernel(part, place, own, *refs):
    first, rest, weights, (sent, kept, lhs, rhs, lhs_sem, rhs_sem) = refs[:2], refs[2], refs[3:11], refs[11:]
    y, zh, z, c = place[0], place[1], place[7], place[8]
    rows, wide = lhs.shape[2], rhs.shape[1]
    cuts = [(lo, min(lo + 256, wide)) for lo in range(0, wide, 256)]
    loads = []
    for n, (lo, hi) in enumerate(cuts):
        loads.append([])
        for d in range(4):
            for u in range(2):
                for f in range(2):
                    k = u * 8 + lax.rem(y + d, 4) * 2 + lax.rem(zh + f, 2)
                    source = weights[f * 4 + d].at[u, :, lo:hi]
                    target = rhs.at[pl.ds(pl.multiple_of(k * 256, 256), 256), lo:hi]
                    loads[n].append(pltpu.make_async_copy(source, target, rhs_sem.at[n * 16 + len(loads[n])]))
    shares = [[], []]
    for group in range(2):
        for i in range(2):
            position = group * 2 + i
            share = place[2 + position]
            for k in range(8):
                shares[group].append((own.at[:, k, part, share], lhs.at[position, :, :, k * 256 : (k + 1) * 256]))
            for d in range(8):
                for e in range(2):
                    core = lax.rem(c + e, 2)
                    source = rest.at[d - 1, core, part, share] if d else first[e].at[part, share]
                    at = lax.rem(z + d, 8)
                    k = 8 + lax.rem(at, 4) * 2 + core
                    target = lhs.at[position, at // 4, :, pl.ds(pl.multiple_of(k * 256, 256), 256)]
                    shares[group].append((source, target))
        shares[group] = [
            pltpu.make_async_copy(source, target, lhs_sem.at[group * 48 + n]) for n, (source, target) in enumerate(shares[group])
        ]
    for copies in (shares[0], loads[0], loads[1], shares[1], *loads[2:]):
        for copy in copies:
            copy.start()
    for group, out in ((0, sent), (1, kept)):
        for copy in shares[group]:
            copy.wait()
        left = lhs[group * 2 : group * 2 + 2].reshape(4 * rows, lhs.shape[3])
        for n, (lo, hi) in enumerate(cuts):
            if group == 0:
                for copy in loads[n]:
                    copy.wait()
            out[:, lo:hi] = jnp.dot(left, rhs[:, lo:hi], preferred_element_type=jnp.float32)


def product(part, place, own, partner, weights):
    rows, wide, depth = own.shape[4], weights[0].shape[2], 4096
    hbm, vmem = pl.BlockSpec(memory_space=pltpu.HBM), pl.BlockSpec(memory_space=pltpu.VMEM)
    operands = [own, *partner, *weights]
    return pl.pallas_call(
        functools.partial(product_kernel, part),
        out_shape=[jax.ShapeDtypeStruct((4 * rows, wide), jnp.float32)] * 2,
        in_specs=[pl.BlockSpec(memory_space=pltpu.SMEM)] + [hbm] * len(operands),
        out_specs=[vmem] * 2,
        scratch_shapes=[
            pltpu.VMEM((4, 2, rows, depth), jnp.bfloat16),
            pltpu.VMEM((depth, wide), jnp.bfloat16),
            pltpu.SemaphoreType.DMA((96,)),
            pltpu.SemaphoreType.DMA((64,)),
        ],
        compiler_params=pltpu.CompilerParams(vmem_limit_bytes=56 << 20),
        cost_estimate=pl.CostEstimate(flops=16 * rows * depth * wide, bytes_accessed=20 << 20, transcendentals=0),
    )(place, *operands)


def pick_kernel(place, panel, out, sem):
    copies = [pltpu.make_async_copy(panel.at[lax.rem(place[7] + 1 + d, 8)], out.at[d], sem.at[d]) for d in range(7)]
    for copy in copies:
        copy.start()
    for copy in copies:
        copy.wait()


def pick(place, panel):
    hbm = pl.BlockSpec(memory_space=pltpu.HBM)
    return pl.pallas_call(
        pick_kernel,
        out_shape=jax.ShapeDtypeStruct((7, *panel.shape[1:]), panel.dtype),
        in_specs=[pl.BlockSpec(memory_space=pltpu.SMEM), hbm],
        out_specs=hbm,
        scratch_shapes=[pltpu.SemaphoreType.DMA((7,))],
        compiler_params=pltpu.CompilerParams(vmem_limit_bytes=56 << 20),
        cost_estimate=pl.CostEstimate(flops=0, bytes_accessed=12 << 20, transcendentals=0),
    )(place, panel)


def cut_kernel(place, gate, up, near, away, give_near, give_away):
    for zh in range(2):
        for q in range(2):

            @pl.when((place[1] == zh) & (place[6] == q))
            def _(zh=zh, q=q):
                for out, half, side_q in ((near, zh, q), (away, 1 - zh, q), (give_near, zh, 1 - q), (give_away, 1 - zh, 1 - q)):
                    base = half * 896
                    for t in range(3):
                        lo = base + side_q * 512 + t * TILE
                        out[:, 2 * t * TILE : (2 * t + 1) * TILE] = gate[:, lo : lo + TILE]
                        out[:, (2 * t + 1) * TILE : (2 * t + 2) * TILE] = up[:, lo : lo + TILE]
                    lo = base + 384 + side_q * 64
                    out[:, 6 * TILE :] = jnp.concatenate([gate[:, lo : lo + 64], up[:, lo : lo + 64]], 1)


def cut(place, gate, up):
    vmem = pl.BlockSpec(memory_space=pltpu.VMEM)
    depth, wide = gate.shape[0], gate.shape[1] // 2
    return pl.pallas_call(
        cut_kernel,
        out_shape=[jax.ShapeDtypeStruct((depth, wide), gate.dtype)] * 4,
        in_specs=[pl.BlockSpec(memory_space=pltpu.SMEM), vmem, vmem],
        out_specs=[vmem] * 4,
        compiler_params=pltpu.CompilerParams(vmem_limit_bytes=24 << 20),
        cost_estimate=pl.CostEstimate(flops=0, bytes_accessed=4 << 20, transcendentals=0),
    )(place, gate, up)


def gated_kernel(place, kept, received, *outs):
    zh = place[1]
    rows = outs[0].shape[0]
    for n, out in enumerate(outs):
        at = pl.multiple_of((n // 2 * 2 + lax.rem(zh + n, 2)) * rows, rows)
        total = kept[pl.ds(at, rows), :] + received[pl.ds(at, rows), :]
        for t in range(3):
            gate, up = total[:, 2 * t * TILE : (2 * t + 1) * TILE], total[:, (2 * t + 1) * TILE : (2 * t + 2) * TILE]
            out[:, t * TILE : (t + 1) * TILE] = (jax.nn.silu(gate) * up).astype(jnp.bfloat16)
        last = total[:, 6 * TILE :]
        up = pltpu.roll(last, TILE // 2, 1)
        out[:, 3 * TILE :] = (jax.nn.silu(last) * up).astype(jnp.bfloat16)[:, : TILE // 2]


def gated(place, kept, received):
    rows, wide = kept.shape
    vmem = pl.BlockSpec(memory_space=pltpu.VMEM)
    return pl.pallas_call(
        gated_kernel,
        out_shape=[jax.ShapeDtypeStruct((rows // 4, wide // 2), jnp.bfloat16)] * 4,
        in_specs=[pl.BlockSpec(memory_space=pltpu.SMEM), vmem, vmem],
        out_specs=[vmem] * 4,
        compiler_params=pltpu.CompilerParams(vmem_limit_bytes=16 << 20),
        cost_estimate=pl.CostEstimate(flops=8 * rows * wide, bytes_accessed=4 << 20, transcendentals=rows * wide // 2),
    )(place, kept, received)


def gather_kernel(place, *refs):
    blocks, out = refs[:8], refs[8]
    rows = blocks[0].shape[0]
    for zh in range(2):
        for q in range(2):

            @pl.when((place[1] == zh) & (place[6] == q))
            def _(zh=zh, q=q):
                for n, block in enumerate(blocks):
                    h, other_q, other_half = n // 4, n // 2 % 2, n % 2
                    at, base = slice(h * rows, (h + 1) * rows), (zh ^ other_half) * 896
                    if q ^ other_q:
                        tile = jnp.concatenate([blocks[n ^ 2][:, 384:], block[:, 384:]], 1)
                        out[at, base + 384 : base + 512] = tile
                        out[at, base + 512 : base + 896] = block[:, :384]
                    else:
                        out[at, base : base + 384] = block[:, :384]


def gather(place, blocks):
    rows = blocks[0].shape[0]
    vmem = pl.BlockSpec(memory_space=pltpu.VMEM)
    return pl.pallas_call(
        gather_kernel,
        out_shape=jax.ShapeDtypeStruct((PARTS * rows, 1792), jnp.bfloat16),
        in_specs=[pl.BlockSpec(memory_space=pltpu.SMEM)] + [vmem] * 8,
        out_specs=vmem,
        compiler_params=pltpu.CompilerParams(vmem_limit_bytes=16 << 20),
        cost_estimate=pl.CostEstimate(flops=0, bytes_accessed=2 << 20, transcendentals=0),
    )(place, *blocks)


def per_device(tokens, gate_weight, up_weight):
    y, zh, x, zl, c = (lax.axis_index(a) for a in AXES)
    ahead = side(x, c)
    partner, summer = (x + ahead + 4) % 4, (x - ahead + 4) % 4
    over = (summer - ahead + 4) % 4
    q = ((x + 1 - c) // 2) % 2
    place = jnp.stack([y, zh, summer, over, x, partner, q, zh * 4 + zl, c]).astype(jnp.int32)
    rows = tokens.shape[0] // NX // PARTS

    split = tokens.reshape(NX, PARTS, rows, 256).swapaxes(0, 1)
    panel = lax.all_gather(split.reshape(PARTS * NX * rows, 256), ("zh", "zl", "c"), axis=0)
    first = [move(split, t) for t in (to_partner, to_crossed)]

    near, away, give_near, give_away = cut(place, gate_weight, up_weight)
    got = move(give_near, to_partner)
    far = [move(away, to_antipode), move(give_away, to_both)]
    near, got, *first = lax.optimization_barrier((near, got, *first))
    near = jnp.stack([near, got])
    near = [near] + [move(near, lambda x, y, z, c, d=d: (x, y - d, z, c)) for d in range(1, 4)]

    panel = lax.optimization_barrier((panel, *far, *near[1:]))[0]
    far = jnp.stack(far)
    far = [far] + [move(far, lambda x, y, z, c, d=d: (x, y - d, z, c)) for d in range(1, 4)]
    own = panel.reshape(2, 8, PARTS, NX, rows, 256)
    rest = move(pick(place, panel.reshape(8, 2, PARTS, NX, rows, 256)), to_partner)

    blocks = []
    for h in range(PARTS):
        sent, kept = product(h, place, own, (*first, rest), (*near, *far))
        parts = gated(place, kept, move(sent, to_summer))
        blocks += [parts[0]] + [move(p, t) for p, t in zip(parts[1:], (to_antipode, to_partner, to_both))]
    return gather(place, blocks)


def solution(mesh):
    fine = Mesh(np.array(mesh.devices).reshape(NY, 2, NX, NZ // 2, NC), AXES)
    rows, cols = ("y", "zh"), ("zl", "c")
    return jax.shard_map(
        per_device,
        mesh=fine,
        in_specs=(P(rows, ("x", *cols)), P(("x", *rows), cols), P(("x", *rows), cols)),
        out_specs=P((*rows, "x"), cols),
        check_vma=False,
    )
```

```python
import functools

import jax
import jax.numpy as jnp
import numpy as np
from jax import lax
from jax.experimental import pallas as pl
from jax.experimental.pallas import tpu as pltpu
from jax.sharding import Mesh
from jax.sharding import PartitionSpec as P

NX, NY, NZ, NC = 4, 4, 8, 2
AXES = ("y", "zh", "x", "zl", "c")
TILE = 128
PARTS = ((0, 512), (512, 896))


def device_index(x, y, z, c):
    return ((y * 2 + z // 4) * NX + x) * 8 + (z % 4) * 2 + c


def side(x, c):
    return 1 - 2 * ((x + c) % 2)


def move(value, target):
    pairs = []
    for x in range(NX):
        for y in range(NY):
            for z in range(NZ):
                for c in range(NC):
                    tx, ty, tz, tc = target(x, y, z, c)
                    pairs.append((device_index(x, y, z, c), device_index(tx % NX, ty % NY, tz % NZ, tc)))
    return lax.ppermute(value, AXES, pairs)


def to_partner(x, y, z, c):
    return x + side(x, c), y, z, c


def to_crossed(x, y, z, c):
    return x + side(x, 1 - c), y, z, 1 - c


def to_antipode(x, y, z, c):
    return x, y, z + 4, c


def to_both(x, y, z, c):
    return x + side(x, c), y, z + 4, c


def to_summer(x, y, z, c):
    return x - side(x, c), y, z, c


def product_kernel(lo, hi, place, own, *refs):
    first, beside, rest, near, far, (out, pieces, lhs, rhs, lhs_sem, rhs_sem) = refs[:2], refs[2:4], refs[4], refs[5:9], refs[9:13], refs[13:]
    y, zh, z, c = place[0], place[1], place[2], place[3]
    rows = pieces.shape[3]
    shares = []
    for i in range(2):
        share, loads = place[6 + i], []
        for k in range(8):
            loads.append((own.at[:, k, share], pieces.at[i, k]))
        for d in range(8):
            for e in range(2):
                core, at = lax.rem(c + e, 2), lax.rem(z + d, 8)
                if d == 0:
                    source = first[e].at[share]
                elif d in (1, 7):
                    source = beside[e].at[d // 7, share]
                else:
                    source = rest.at[d - 2, core, share]
                loads.append((source, pieces.at[i, 8 + lax.rem(at, 4) * 2 + core, at // 4]))
        shares.append([pltpu.make_async_copy(a, b, lhs_sem.at[i * 24 + n]) for n, (a, b) in enumerate(loads)])
    weights = []
    for d in range(4):
        for u in range(2):
            for f in range(2):
                k = u * 8 + lax.rem(y + d, 4) * 2 + lax.rem(zh + f, 2)
                source = far[d].at[u] if f else near[d].at[u, :, lo:hi]
                target = rhs.at[pl.ds(pl.multiple_of(k * 256, 256), 256)]
                weights.append(pltpu.make_async_copy(source, target, rhs_sem.at[len(weights)]))
    for copy in (*shares[0], *weights, *shares[1]):
        copy.start()
    for i in range(2):
        for copy in shares[i]:
            copy.wait()
        for k in range(16):
            lhs[:, k * 256 : (k + 1) * 256] = pieces[i, k].reshape(2 * rows, 256)
        if i == 0:
            for copy in weights:
                copy.wait()
        for at in range(0, hi - lo, 256):
            to = min(at + 256, hi - lo)
            out[i * 2 * rows : (i + 1) * 2 * rows, at:to] = jnp.dot(lhs[...], rhs[:, at:to], preferred_element_type=jnp.float32)


def product(part, place, own, partner, near, far):
    lo, hi = part
    rows, depth = own.shape[3], 4096
    hbm, vmem = pl.BlockSpec(memory_space=pltpu.HBM), pl.BlockSpec(memory_space=pltpu.VMEM)
    operands = [own, *partner, *near, *far]
    return pl.pallas_call(
        functools.partial(product_kernel, lo, hi),
        out_shape=jax.ShapeDtypeStruct((4 * rows, hi - lo), jnp.float32),
        in_specs=[pl.BlockSpec(memory_space=pltpu.SMEM)] + [hbm] * len(operands),
        out_specs=vmem,
        scratch_shapes=[
            pltpu.VMEM((2, 16, 2, rows, 256), jnp.bfloat16),
            pltpu.VMEM((2 * rows, depth), jnp.bfloat16),
            pltpu.VMEM((depth, hi - lo), jnp.bfloat16),
            pltpu.SemaphoreType.DMA((48,)),
            pltpu.SemaphoreType.DMA((16,)),
        ],
        compiler_params=pltpu.CompilerParams(vmem_limit_bytes=48 << 20),
        cost_estimate=pl.CostEstimate(flops=8 * rows * depth * (hi - lo), bytes_accessed=12 << 20, transcendentals=0),
    )(place, *operands)


def pick_kernel(place, panel, out, sem):
    copies = [pltpu.make_async_copy(panel.at[lax.rem(place[2] + 2 + d, 8)], out.at[d], sem.at[d]) for d in range(5)]
    for copy in copies:
        copy.start()
    for copy in copies:
        copy.wait()


def pick(place, panel):
    return pl.pallas_call(
        pick_kernel,
        out_shape=jax.ShapeDtypeStruct((5, *panel.shape[1:]), panel.dtype),
        in_specs=[pl.BlockSpec(memory_space=pltpu.SMEM), pl.BlockSpec(memory_space=pltpu.HBM)],
        out_specs=pl.BlockSpec(memory_space=pltpu.VMEM),
        scratch_shapes=[pltpu.SemaphoreType.DMA((5,))],
        compiler_params=pltpu.CompilerParams(vmem_limit_bytes=16 << 20),
        cost_estimate=pl.CostEstimate(flops=0, bytes_accessed=8 << 20, transcendentals=0),
    )(place, panel)


def cut_kernel(place, gate, up, near, away, give):
    for zh in range(2):
        for q in range(2):

            @pl.when((place[1] == zh) & (place[8] == q))
            def _(zh=zh, q=q):
                for out, half, side_q in ((near, zh, q), (away, 1 - zh, q), (give.at[0], zh, 1 - q), (give.at[1], 1 - zh, 1 - q)):
                    base = half * 896
                    for t in range(3):
                        lo = base + side_q * 512 + t * TILE
                        out[:, 2 * t * TILE : (2 * t + 1) * TILE] = gate[:, lo : lo + TILE]
                        out[:, (2 * t + 1) * TILE : (2 * t + 2) * TILE] = up[:, lo : lo + TILE]
                    lo = base + 384 + side_q * 64
                    out[:, 6 * TILE :] = jnp.concatenate([gate[:, lo : lo + 64], up[:, lo : lo + 64]], 1)


def cut(place, gate, up):
    vmem = pl.BlockSpec(memory_space=pltpu.VMEM)
    depth, wide = gate.shape[0], gate.shape[1] // 2
    return pl.pallas_call(
        cut_kernel,
        out_shape=[jax.ShapeDtypeStruct((depth, wide), gate.dtype)] * 2 + [jax.ShapeDtypeStruct((2, depth, wide), gate.dtype)],
        in_specs=[pl.BlockSpec(memory_space=pltpu.SMEM), vmem, vmem],
        out_specs=[vmem] * 3,
        compiler_params=pltpu.CompilerParams(vmem_limit_bytes=24 << 20),
        cost_estimate=pl.CostEstimate(flops=0, bytes_accessed=4 << 20, transcendentals=0),
    )(place, gate, up)


def gated_kernel(place, kept, received, *outs):
    zh = place[1]
    rows = outs[0].shape[0]
    for n, out in enumerate(outs):
        at = pl.multiple_of((n // 2 * 2 + lax.rem(zh + n, 2)) * rows, rows)
        total = kept[pl.ds(at, rows), :] + received[pl.ds(at, rows), :]
        whole = total.shape[1] // (2 * TILE)
        for t in range(whole):
            gate, up = total[:, 2 * t * TILE : (2 * t + 1) * TILE], total[:, (2 * t + 1) * TILE : (2 * t + 2) * TILE]
            out[:, t * TILE : (t + 1) * TILE] = (jax.nn.silu(gate) * up).astype(jnp.bfloat16)
        if total.shape[1] % (2 * TILE):
            last = total[:, 2 * whole * TILE :]
            up = pltpu.roll(last, TILE // 2, 1)
            out[:, whole * TILE :] = (jax.nn.silu(last) * up).astype(jnp.bfloat16)[:, : TILE // 2]


def gated(place, kept, received):
    rows, wide = kept.shape
    vmem = pl.BlockSpec(memory_space=pltpu.VMEM)
    return pl.pallas_call(
        gated_kernel,
        out_shape=[jax.ShapeDtypeStruct((rows // 4, wide // 2), jnp.bfloat16)] * 4,
        in_specs=[pl.BlockSpec(memory_space=pltpu.SMEM), vmem, vmem],
        out_specs=[vmem] * 4,
        compiler_params=pltpu.CompilerParams(vmem_limit_bytes=16 << 20),
        cost_estimate=pl.CostEstimate(flops=8 * rows * wide, bytes_accessed=4 << 20, transcendentals=rows * wide // 2),
    )(place, kept, received)


def gather_kernel(place, *refs):
    blocks, out = refs[:8], refs[8]
    for zh in range(2):
        for q in range(2):

            @pl.when((place[1] == zh) & (place[8] == q))
            def _(zh=zh, q=q):
                for other in range(2):
                    base = (zh ^ other) * 896
                    for side_q in range(2):
                        n = 2 * (q ^ side_q) + other
                        at = base + side_q * 512
                        out[:, at : at + 256] = blocks[n][...]
                        out[:, at + 256 : at + 384] = blocks[4 + n][:, :TILE]
                    halves = [blocks[4 + 2 * (q ^ side_q) + other][:, TILE:] for side_q in range(2)]
                    out[:, base + 384 : base + 512] = jnp.concatenate(halves, 1)


def gather(place, blocks):
    vmem = pl.BlockSpec(memory_space=pltpu.VMEM)
    return pl.pallas_call(
        gather_kernel,
        out_shape=jax.ShapeDtypeStruct((blocks[0].shape[0], 1792), jnp.bfloat16),
        in_specs=[pl.BlockSpec(memory_space=pltpu.SMEM)] + [vmem] * 8,
        out_specs=vmem,
        compiler_params=pltpu.CompilerParams(vmem_limit_bytes=16 << 20),
        cost_estimate=pl.CostEstimate(flops=0, bytes_accessed=2 << 20, transcendentals=0),
    )(place, *blocks)


def along_y(value):
    return [value] + [move(value, lambda x, y, z, c, d=d: (x, y - d, z, c)) for d in range(1, 4)]


def after(value, *others):
    return lax.optimization_barrier((value, *others))[0]


def per_device(tokens, gate_weight, up_weight):
    y, zh, x, zl, c = (lax.axis_index(a) for a in AXES)
    ahead = side(x, c)
    partner, summer = (x + ahead + 4) % 4, (x - ahead + 4) % 4
    over = (summer - ahead + 4) % 4
    q = ((x + 1 - c) // 2) % 2
    rows = tokens.shape[0] // NX

    def places(a, b):
        return jnp.stack([y, zh, zh * 4 + zl, c, x, partner, a, b, q]).astype(jnp.int32)

    send_place, keep_place = places(summer, over), places(x, partner)

    panel = lax.all_gather(tokens, ("zh", "zl", "c"), axis=0)
    split = tokens.reshape(NX, rows, 256)
    around = [move(split, lambda x, y, z, c: (x, y, z - 1, c)), move(split, lambda x, y, z, c: (x, y, z + 1, c))]
    first = [move(split, t) for t in (to_partner, to_crossed)]
    near, away, give = cut(keep_place, gate_weight, up_weight)
    got = move(give, to_partner)

    near, away, got, around, first = lax.optimization_barrier((near, away, got, around, first))
    far = [jnp.stack([away[:, lo:hi], got[1, :, lo:hi]]) for lo, hi in PARTS]
    far[0] = move(far[0], to_antipode)
    near = along_y(jnp.stack([near, got[0]]))
    around = jnp.stack(around)
    beside = [move(around, t) for t in (to_partner, to_crossed)]

    panel = after(panel, far[0], *near[1:], *beside)
    own = panel.reshape(2, 8, NX, rows, 256)
    rest = move(pick(keep_place, panel.reshape(8, 2, NX, rows, 256)), to_partner)
    far[1] = move(after(far[1], panel), to_antipode)
    far = [along_y(f) for f in far]

    held = (*first, *beside, rest)
    sums = [move(product(p, send_place, own, held, near, f), to_summer) for p, f in zip(PARTS, far)]
    blocks = []
    for p, f, received in zip(PARTS, far, sums):
        turn = after(keep_place, *blocks[:1])
        parts = gated(keep_place, product(p, turn, own, held, near, f), received)
        blocks += [parts[0]] + [move(b, t) for b, t in zip(parts[1:], (to_antipode, to_partner, to_both))]
    return gather(keep_place, blocks)


def solution(mesh):
    fine = Mesh(np.array(mesh.devices).reshape(NY, 2, NX, NZ // 2, NC), AXES)
    rows, cols = ("y", "zh"), ("zl", "c")
    return jax.shard_map(
        per_device,
        mesh=fine,
        in_specs=(P(rows, ("x", *cols)), P(("x", *rows), cols), P(("x", *rows), cols)),
        out_specs=P((*rows, "x"), cols),
        check_vma=False,
    )
```

```python
import functools

import jax
import jax.numpy as jnp
import numpy as np
from jax import lax
from jax.experimental import pallas as pl
from jax.experimental.pallas import tpu as pltpu
from jax.sharding import Mesh
from jax.sharding import PartitionSpec as P

NX, NY, NZ, NC = 4, 4, 8, 2
AXES = ("y", "zh", "x", "zl", "c")
TILE = 128
PARTS = ((0, 512), (512, 896))


def device_index(x, y, z, c):
    return ((y * 2 + z // 4) * NX + x) * 8 + (z % 4) * 2 + c


def side(x, c):
    return 1 - 2 * ((x + c) % 2)


def move(value, target):
    pairs = []
    for x in range(NX):
        for y in range(NY):
            for z in range(NZ):
                for c in range(NC):
                    tx, ty, tz, tc = target(x, y, z, c)
                    pairs.append((device_index(x, y, z, c), device_index(tx % NX, ty % NY, tz % NZ, tc)))
    return lax.ppermute(value, AXES, pairs)


def to_partner(x, y, z, c):
    return x + side(x, c), y, z, c


def to_crossed(x, y, z, c):
    return x + side(x, 1 - c), y, z, 1 - c


def to_antipode(x, y, z, c):
    return x, y, z + 4, c


def to_both(x, y, z, c):
    return x + side(x, c), y, z + 4, c


def to_summer(x, y, z, c):
    return x - side(x, c), y, z, c


def product_kernel(place, own, partner, *refs):
    near, far, (outs, lhs, rhs) = refs[:4], (refs[4:8], refs[8:12]), (refs[12:14], *refs[14:])
    y, zh = place[0], place[1]
    rows = own.shape[3]
    for d in range(4):
        for u in range(2):
            k = u * 8 + lax.rem(y + d, 4) * 2
            at = pl.ds(pl.multiple_of((k + zh) * 256, 256), 256)
            rhs[at, :] = near[d][u]
            at = pl.ds(pl.multiple_of((k + 1 - zh) * 256, 256), 256)
            for (lo, hi), part in zip(PARTS, far):
                rhs[at, lo:hi] = part[d][u]
    for i, out in enumerate(outs):
        for k in range(16):
            source = own if k < 8 else partner
            lhs[:, k * 256 : (k + 1) * 256] = source[:, k % 8, place[4 + i]].reshape(2 * rows, 256)
        for at in range(0, rhs.shape[1], 256):
            to = min(at + 256, rhs.shape[1])
            out[:, at:to] = jnp.dot(lhs[...], rhs[:, at:to], preferred_element_type=jnp.float32)


def product(place, own, partner, near, far):
    rows, depth, wide = own.shape[3], 4096, near[0].shape[2]
    vmem = pl.BlockSpec(memory_space=pltpu.VMEM)
    operands = [own, partner, *near, *far[0], *far[1]]
    return pl.pallas_call(
        product_kernel,
        out_shape=[jax.ShapeDtypeStruct((2 * rows, wide), jnp.float32)] * 2,
        in_specs=[pl.BlockSpec(memory_space=pltpu.SMEM)] + [vmem] * len(operands),
        out_specs=[vmem] * 2,
        scratch_shapes=[pltpu.VMEM((2 * rows, depth), jnp.bfloat16), pltpu.VMEM((depth, wide), jnp.bfloat16)],
        compiler_params=pltpu.CompilerParams(vmem_limit_bytes=40 << 20),
        cost_estimate=pl.CostEstimate(flops=8 * rows * depth * wide, bytes_accessed=24 << 20, transcendentals=0),
    )(place, *operands)


def cut_kernel(place, gate, up, near, away, give_near, give_away):
    for zh in range(2):
        for q in range(2):

            @pl.when((place[1] == zh) & (place[6] == q))
            def _(zh=zh, q=q):
                for out, half, side_q in ((near, zh, q), (away, 1 - zh, q), (give_near, zh, 1 - q), (give_away, 1 - zh, 1 - q)):
                    base = half * 896
                    for t in range(3):
                        lo = base + side_q * 512 + t * TILE
                        out[:, 2 * t * TILE : (2 * t + 1) * TILE] = gate[:, lo : lo + TILE]
                        out[:, (2 * t + 1) * TILE : (2 * t + 2) * TILE] = up[:, lo : lo + TILE]
                    lo = base + 384 + side_q * 64
                    out[:, 6 * TILE :] = jnp.concatenate([gate[:, lo : lo + 64], up[:, lo : lo + 64]], 1)


def cut(place, gate, up):
    vmem = pl.BlockSpec(memory_space=pltpu.VMEM)
    depth, wide = gate.shape[0], gate.shape[1] // 2
    return pl.pallas_call(
        cut_kernel,
        out_shape=[jax.ShapeDtypeStruct((depth, wide), gate.dtype)] * 4,
        in_specs=[pl.BlockSpec(memory_space=pltpu.SMEM), vmem, vmem],
        out_specs=[vmem] * 4,
        compiler_params=pltpu.CompilerParams(vmem_limit_bytes=24 << 20),
        cost_estimate=pl.CostEstimate(flops=0, bytes_accessed=4 << 20, transcendentals=0),
    )(place, gate, up)


def gated_kernel(place, kept, received, *outs):
    zh = place[1]
    rows, whole = outs[0].shape[0], kept.shape[1] // (2 * TILE)
    for n, out in enumerate(outs):
        at = pl.ds(pl.multiple_of(lax.rem(zh + n, 2) * rows, rows), rows)
        total = kept[at, :] + received[at, :]
        for t in range(whole):
            gate, up = total[:, 2 * t * TILE : (2 * t + 1) * TILE], total[:, (2 * t + 1) * TILE : (2 * t + 2) * TILE]
            out[:, t * TILE : (t + 1) * TILE] = (jax.nn.silu(gate) * up).astype(jnp.bfloat16)
        last = total[:, 2 * whole * TILE :]
        up = pltpu.roll(last, TILE // 2, 1)
        out[:, whole * TILE :] = (jax.nn.silu(last) * up).astype(jnp.bfloat16)[:, : TILE // 2]


def gated(place, kept, received):
    rows, wide = kept.shape
    vmem = pl.BlockSpec(memory_space=pltpu.VMEM)
    return pl.pallas_call(
        gated_kernel,
        out_shape=[jax.ShapeDtypeStruct((rows // 2, wide // 2), jnp.bfloat16)] * 2,
        in_specs=[pl.BlockSpec(memory_space=pltpu.SMEM), vmem, vmem],
        out_specs=[vmem] * 2,
        compiler_params=pltpu.CompilerParams(vmem_limit_bytes=16 << 20),
        cost_estimate=pl.CostEstimate(flops=8 * rows * wide, bytes_accessed=4 << 20, transcendentals=rows * wide // 2),
    )(place, kept, received)


def gather_kernel(place, *refs):
    blocks, out = refs[:4], refs[4]
    for zh in range(2):
        for q in range(2):

            @pl.when((place[1] == zh) & (place[6] == q))
            def _(zh=zh, q=q):
                for other in range(2):
                    base = (zh ^ other) * 896
                    low, high = blocks[2 * q + other], blocks[2 * (1 - q) + other]
                    out[:, base : base + 384] = low[:, :384]
                    out[:, base + 384 : base + 512] = jnp.concatenate([low[:, 384:], high[:, 384:]], 1)
                    out[:, base + 512 : base + 896] = high[:, :384]


def gather(place, blocks):
    vmem = pl.BlockSpec(memory_space=pltpu.VMEM)
    return pl.pallas_call(
        gather_kernel,
        out_shape=jax.ShapeDtypeStruct((blocks[0].shape[0], 1792), jnp.bfloat16),
        in_specs=[pl.BlockSpec(memory_space=pltpu.SMEM)] + [vmem] * 4,
        out_specs=vmem,
        compiler_params=pltpu.CompilerParams(vmem_limit_bytes=16 << 20),
        cost_estimate=pl.CostEstimate(flops=0, bytes_accessed=2 << 20, transcendentals=0),
    )(place, *blocks)


def along_y(value):
    return [value] + [move(value, lambda x, y, z, c, d=d: (x, y - d, z, c)) for d in range(1, 4)]


def after(value, *others):
    return lax.optimization_barrier((value, *others))[0]


def per_device(tokens, gate_weight, up_weight):
    y, zh, x, zl, c = (lax.axis_index(a) for a in AXES)
    ahead = side(x, c)
    partner, summer = (x + ahead + 4) % 4, (x - ahead + 4) % 4
    over = (summer - ahead + 4) % 4
    q = ((x + 1 - c) // 2) % 2
    rows = tokens.shape[0] // NX

    def places(a, b):
        return jnp.stack([y, zh, zl, c, a, b, q]).astype(jnp.int32)

    send_place, keep_place = places(summer, over), places(x, partner)

    panel = lax.all_gather(tokens, ("zh", "zl", "c"), axis=0)
    near, away, give_near, give_away = cut(keep_place, gate_weight, up_weight)
    got_near, got_away = move(give_near, to_partner), move(give_away, to_partner)
    near = along_y(jnp.stack([near, got_near]))

    panel = after(panel, got_away, *near[1:])
    partner_panel = move(panel, to_partner).reshape(2, 8, NX, rows, 256)
    own = panel.reshape(2, 8, NX, rows, 256)
    away, got_away = lax.optimization_barrier((away, got_away, panel))[:2]
    far = [jnp.stack([away[:, lo:hi], got_away[:, lo:hi]]) for lo, hi in PARTS]
    far[0] = move(far[0], to_antipode)
    far[1] = move(after(far[1], far[0]), to_antipode)
    far = [along_y(f) for f in far]

    sent = product(send_place, own, partner_panel, near, far)
    sums = [move(sent[0], to_summer), move(sent[1], to_summer)]
    kept = product(after(keep_place, *sent), own, partner_panel, near, far)
    mine, over_z = gated(keep_place, kept[0], sums[0])
    over_x, over_both = gated(keep_place, kept[1], sums[1])
    blocks = [mine, move(over_z, to_antipode), move(over_x, to_partner), move(over_both, to_both)]
    return gather(keep_place, blocks)


def solution(mesh):
    fine = Mesh(np.array(mesh.devices).reshape(NY, 2, NX, NZ // 2, NC), AXES)
    rows, cols = ("y", "zh"), ("zl", "c")
    return jax.shard_map(
        per_device,
        mesh=fine,
        in_specs=(P(rows, ("x", *cols)), P(("x", *rows), cols), P(("x", *rows), cols)),
        out_specs=P((*rows, "x"), cols),
        check_vma=False,
    )
```

```python
import functools

import jax
import jax.numpy as jnp
import numpy as np
from jax import lax
from jax.experimental import pallas as pl
from jax.experimental.pallas import tpu as pltpu
from jax.sharding import Mesh
from jax.sharding import PartitionSpec as P

NX, NY, NZ, NC = 4, 4, 8, 2
AXES = ("y", "zh", "x", "zl", "c")
TILE = 128
STEPS = ((0,), (1, 7), (2, 6), (3, 5), (4,))
PARTS = ((0, 512), (512, 896))


def device_index(x, y, z, c):
    return ((y * 2 + z // 4) * NX + x) * 8 + (z % 4) * 2 + c


def side(x, c):
    return 1 - 2 * ((x + c) % 2)


def move(value, target):
    pairs = []
    for x in range(NX):
        for y in range(NY):
            for z in range(NZ):
                for c in range(NC):
                    tx, ty, tz, tc = target(x, y, z, c)
                    pairs.append((device_index(x, y, z, c), device_index(tx % NX, ty % NY, tz % NZ, tc)))
    return lax.ppermute(value, AXES, pairs)


def to_partner(x, y, z, c):
    return x + side(x, c), y, z, c


def to_crossed(x, y, z, c):
    return x + side(x, 1 - c), y, z, 1 - c


def to_antipode(x, y, z, c):
    return x, y, z + 4, c


def to_both(x, y, z, c):
    return x + side(x, c), y, z + 4, c


def to_summer(x, y, z, c):
    return x - side(x, c), y, z, c


def product_kernel(place, *refs):
    tokens, near, far = refs[:20], refs[20], (refs[21:25], refs[25:29])
    outs, (pieces, lhs, rhs, lhs_sem, rhs_sem) = refs[29:31], refs[31:]
    y, zh, zl, c = place[0], place[1], place[2], place[3]
    rows = pieces.shape[3]
    shares = []
    for i in range(2):
        loads = []
        for s, offsets in enumerate(STEPS):
            for j, d in enumerate(offsets):
                z = lax.rem(zh * 4 + zl + d, 8)
                for t in range(4):
                    k = t // 2 * 8 + lax.rem(z, 4) * 2 + lax.rem(c + t, 2)
                    source, target = tokens[4 * s + t].at[j, place[4 + i]], pieces.at[i, k, z // 4]
                    loads.append(pltpu.make_async_copy(source, target, lhs_sem.at[i * 32 + len(loads)]))
        shares.append(loads)
    weights = []
    for d in range(4):
        for u in range(2):
            at = pl.multiple_of((u * 8 + d * 2 + zh) * 256, 256)
            weights.append(pltpu.make_async_copy(near.at[d, u], rhs.at[pl.ds(at, 256)], rhs_sem.at[len(weights)]))
            at = pl.multiple_of((u * 8 + lax.rem(y + d, 4) * 2 + 1 - zh) * 256, 256)
            for (lo, hi), part in zip(PARTS, far):
                target = rhs.at[pl.ds(at, 256), lo:hi]
                weights.append(pltpu.make_async_copy(part[d].at[u], target, rhs_sem.at[len(weights)]))
    for copy in (*shares[0], *weights, *shares[1]):
        copy.start()
    for i, out in enumerate(outs):
        for copy in shares[i]:
            copy.wait()
        for k in range(16):
            lhs[:, k * 256 : (k + 1) * 256] = pieces[i, k].reshape(2 * rows, 256)
        if i == 0:
            for copy in weights:
                copy.wait()
        for at in range(0, rhs.shape[1], 256):
            to = min(at + 256, rhs.shape[1])
            out[:, at:to] = jnp.dot(lhs[...], rhs[:, at:to], preferred_element_type=jnp.float32)


def product(place, tokens, near, far):
    rows, depth, wide = tokens[0].shape[2], 4096, near.shape[3]
    hbm, vmem = pl.BlockSpec(memory_space=pltpu.HBM), pl.BlockSpec(memory_space=pltpu.VMEM)
    operands = [*tokens, near, *far[0], *far[1]]
    return pl.pallas_call(
        product_kernel,
        out_shape=[jax.ShapeDtypeStruct((2 * rows, wide), jnp.float32)] * 2,
        in_specs=[pl.BlockSpec(memory_space=pltpu.SMEM)] + [hbm] * len(operands),
        out_specs=[vmem] * 2,
        scratch_shapes=[
            pltpu.VMEM((2, 16, 2, rows, 256), jnp.bfloat16),
            pltpu.VMEM((2 * rows, depth), jnp.bfloat16),
            pltpu.VMEM((depth, wide), jnp.bfloat16),
            pltpu.SemaphoreType.DMA((64,)),
            pltpu.SemaphoreType.DMA((24,)),
        ],
        compiler_params=pltpu.CompilerParams(vmem_limit_bytes=60 << 20),
        cost_estimate=pl.CostEstimate(flops=8 * rows * depth * wide, bytes_accessed=24 << 20, transcendentals=0),
    )(place, *operands)


def cut_kernel(place, gate, up, near, away, give_near, give_away):
    for zh in range(2):
        for q in range(2):

            @pl.when((place[1] == zh) & (place[6] == q))
            def _(zh=zh, q=q):
                for out, half, side_q in ((near, zh, q), (away, 1 - zh, q), (give_near, zh, 1 - q), (give_away, 1 - zh, 1 - q)):
                    base = half * 896
                    for t in range(3):
                        lo = base + side_q * 512 + t * TILE
                        out[:, 2 * t * TILE : (2 * t + 1) * TILE] = gate[:, lo : lo + TILE]
                        out[:, (2 * t + 1) * TILE : (2 * t + 2) * TILE] = up[:, lo : lo + TILE]
                    lo = base + 384 + side_q * 64
                    out[:, 6 * TILE :] = jnp.concatenate([gate[:, lo : lo + 64], up[:, lo : lo + 64]], 1)


def cut(place, gate, up):
    vmem = pl.BlockSpec(memory_space=pltpu.VMEM)
    depth, wide = gate.shape[0], gate.shape[1] // 2
    return pl.pallas_call(
        cut_kernel,
        out_shape=[jax.ShapeDtypeStruct((depth, wide), gate.dtype)] * 4,
        in_specs=[pl.BlockSpec(memory_space=pltpu.SMEM), vmem, vmem],
        out_specs=[vmem] * 4,
        compiler_params=pltpu.CompilerParams(vmem_limit_bytes=24 << 20),
        cost_estimate=pl.CostEstimate(flops=0, bytes_accessed=4 << 20, transcendentals=0),
    )(place, gate, up)


def gated_kernel(place, kept, received, *outs):
    zh = place[1]
    rows, whole = outs[0].shape[0], kept.shape[1] // (2 * TILE)
    for n, out in enumerate(outs):
        at = pl.ds(pl.multiple_of(lax.rem(zh + n, 2) * rows, rows), rows)
        total = kept[at, :] + received[at, :]
        for t in range(whole):
            gate, up = total[:, 2 * t * TILE : (2 * t + 1) * TILE], total[:, (2 * t + 1) * TILE : (2 * t + 2) * TILE]
            out[:, t * TILE : (t + 1) * TILE] = (jax.nn.silu(gate) * up).astype(jnp.bfloat16)
        last = total[:, 2 * whole * TILE :]
        up = pltpu.roll(last, TILE // 2, 1)
        out[:, whole * TILE :] = (jax.nn.silu(last) * up).astype(jnp.bfloat16)[:, : TILE // 2]


def gated(place, kept, received):
    rows, wide = kept.shape
    vmem = pl.BlockSpec(memory_space=pltpu.VMEM)
    return pl.pallas_call(
        gated_kernel,
        out_shape=[jax.ShapeDtypeStruct((rows // 2, wide // 2), jnp.bfloat16)] * 2,
        in_specs=[pl.BlockSpec(memory_space=pltpu.SMEM), vmem, vmem],
        out_specs=[vmem] * 2,
        compiler_params=pltpu.CompilerParams(vmem_limit_bytes=16 << 20),
        cost_estimate=pl.CostEstimate(flops=8 * rows * wide, bytes_accessed=4 << 20, transcendentals=rows * wide // 2),
    )(place, kept, received)


def gather_kernel(place, *refs):
    blocks, out = refs[:4], refs[4]
    for zh in range(2):
        for q in range(2):

            @pl.when((place[1] == zh) & (place[6] == q))
            def _(zh=zh, q=q):
                for other in range(2):
                    base = (zh ^ other) * 896
                    low, high = blocks[2 * q + other], blocks[2 * (1 - q) + other]
                    out[:, base : base + 384] = low[:, :384]
                    out[:, base + 384 : base + 512] = jnp.concatenate([low[:, 384:], high[:, 384:]], 1)
                    out[:, base + 512 : base + 896] = high[:, :384]


def gather(place, blocks):
    vmem = pl.BlockSpec(memory_space=pltpu.VMEM)
    return pl.pallas_call(
        gather_kernel,
        out_shape=jax.ShapeDtypeStruct((blocks[0].shape[0], 1792), jnp.bfloat16),
        in_specs=[pl.BlockSpec(memory_space=pltpu.SMEM)] + [vmem] * 4,
        out_specs=vmem,
        compiler_params=pltpu.CompilerParams(vmem_limit_bytes=16 << 20),
        cost_estimate=pl.CostEstimate(flops=0, bytes_accessed=2 << 20, transcendentals=0),
    )(place, *blocks)


def along_y(value):
    return [value] + [move(value, lambda x, y, z, c, d=d: (x, y - d, z, c)) for d in range(1, 4)]


def after(value, *others):
    return lax.optimization_barrier((value, *others))[0]


def per_device(tokens, gate_weight, up_weight):
    y, zh, x, zl, c = (lax.axis_index(a) for a in AXES)
    ahead = side(x, c)
    partner, summer = (x + ahead + 4) % 4, (x - ahead + 4) % 4
    over = (summer - ahead + 4) % 4
    q = ((x + 1 - c) // 2) % 2
    rows = tokens.shape[0] // NX

    def places(a, b):
        return jnp.stack([y, zh, zl, c, a, b, q]).astype(jnp.int32)

    send_place, keep_place = places(summer, over), places(x, partner)

    near, away, give_near, give_away = cut(keep_place, gate_weight, up_weight)
    got_near, got_away = move(give_near, to_partner), move(give_away, to_partner)
    far = [jnp.stack([away[:, lo:hi], got_away[:, lo:hi]]) for lo, hi in PARTS]
    far[0] = move(far[0], to_antipode)

    block = tokens.reshape(1, NX, rows, 256)
    held, sent_on = [], ()
    behind = before = block
    for s in range(5):
        if s in (1, 2, 3):
            behind = move(behind, lambda x, y, z, c: (x, y, z - 1, c))
            before = move(before, lambda x, y, z, c: (x, y, z + 1, c))
            block = jnp.concatenate([behind, before])
        elif s == 4:
            block = move(jnp.where(c == 0, before, behind), lambda x, y, z, c: (x, y, z + 1 - 2 * c, c))
        ready = after(block, *sent_on, *far[: s // 3])
        sent_on = [move(ready, to_partner), move(ready, to_crossed)]
        held += [block, move(ready, lambda x, y, z, c: (x, y, z, 1 - c)), *sent_on]

    near = lax.all_gather(jnp.stack([near, got_near]), "y", axis=0)
    far[1] = move(after(far[1], far[0]), to_antipode)
    far = [along_y(f) for f in far]

    sent = product(send_place, held, near, far)
    sums = [move(sent[0], to_summer), move(sent[1], to_summer)]
    kept = product(after(keep_place, *sent), held, near, far)
    mine, over_z = gated(keep_place, kept[0], sums[0])
    over_x, over_both = gated(keep_place, kept[1], sums[1])
    blocks = [mine, move(over_z, to_antipode), move(over_x, to_partner), move(over_both, to_both)]
    return gather(keep_place, blocks)


def solution(mesh):
    fine = Mesh(np.array(mesh.devices).reshape(NY, 2, NX, NZ // 2, NC), AXES)
    rows, cols = ("y", "zh"), ("zl", "c")
    return jax.shard_map(
        per_device,
        mesh=fine,
        in_specs=(P(rows, ("x", *cols)), P(("x", *rows), cols), P(("x", *rows), cols)),
        out_specs=P((*rows, "x"), cols),
        check_vma=False,
    )
```

```python
import functools

import jax
import jax.numpy as jnp
import numpy as np
from jax import lax
from jax.experimental import pallas as pl
from jax.experimental.pallas import tpu as pltpu
from jax.sharding import Mesh
from jax.sharding import PartitionSpec as P

NX, NY, NZ, NC = 4, 4, 8, 2
AXES = ("y", "zh", "x", "zl", "c")
TILE = 128
PARTS = ((0, 512), (512, 896))


def device_index(x, y, z, c):
    return ((y * 2 + z // 4) * NX + x) * 8 + (z % 4) * 2 + c


def side(x, c):
    return 1 - 2 * ((x + c) % 2)


def move(value, target):
    pairs = []
    for x in range(NX):
        for y in range(NY):
            for z in range(NZ):
                for c in range(NC):
                    tx, ty, tz, tc = target(x, y, z, c)
                    pairs.append((device_index(x, y, z, c), device_index(tx % NX, ty % NY, tz % NZ, tc)))
    return lax.ppermute(value, AXES, pairs)


def to_partner(x, y, z, c):
    return x + side(x, c), y, z, c


def to_crossed(x, y, z, c):
    return x + side(x, 1 - c), y, z, 1 - c


def to_antipode(x, y, z, c):
    return x, y, z + 4, c


def to_both(x, y, z, c):
    return x + side(x, c), y, z + 4, c


def to_summer(x, y, z, c):
    return x - side(x, c), y, z, c


def product_kernel(u, place, panel, *refs):
    near, far, refs = refs[:4], (refs[4:8], refs[8:12]), refs[12:]
    before, (outs, pieces, lhs, rhs, lhs_sem, rhs_sem) = refs[: 2 * u], (refs[2 * u : 2 * u + 2], *refs[2 * u + 2 :])
    y, zh = place[0], place[1]
    rows, wide = lhs.shape[0] // 4, rhs.shape[1]
    tokens = [pltpu.make_async_copy(panel.at[:, :, place[4 + i]], pieces.at[i], lhs_sem.at[i]) for i in range(2)]
    weights = []
    for d in range(4):
        k = lax.rem(y + d, 4) * 2
        at = pl.multiple_of((k + zh) * 256, 256)
        weights.append(pltpu.make_async_copy(near[d].at[u], rhs.at[pl.ds(at, 256)], rhs_sem.at[d * 3]))
        at = pl.multiple_of((k + 1 - zh) * 256, 256)
        for n, ((lo, hi), part) in enumerate(zip(PARTS, far)):
            target = rhs.at[pl.ds(at, 256), lo:hi]
            weights.append(pltpu.make_async_copy(part[d].at[u], target, rhs_sem.at[d * 3 + 1 + n]))
    for copy in (*tokens, *weights):
        copy.start()
    for i in range(2):
        tokens[i].wait()
        for b in range(2):
            at = (i * 2 + b) * rows
            for k in range(8):
                lhs[at : at + rows, k * 256 : (k + 1) * 256] = pieces[i, b, k]
    for copy in weights:
        copy.wait()
    for lo in range(0, wide, 256):
        hi = min(lo + 256, wide)
        part = jnp.dot(lhs[...], rhs[:, lo:hi], preferred_element_type=jnp.float32)
        for i, out in enumerate(outs):
            mine = part[i * 2 * rows : (i + 1) * 2 * rows]
            out[:, lo:hi] = before[i][:, lo:hi] + mine if u else mine


def product(u, place, panel, near, far, before=()):
    rows, depth, wide = panel.shape[3], 2048, near[0].shape[2]
    hbm, vmem = pl.BlockSpec(memory_space=pltpu.HBM), pl.BlockSpec(memory_space=pltpu.VMEM)
    operands = [panel, *near, *far[0], *far[1]]
    return pl.pallas_call(
        functools.partial(product_kernel, u),
        out_shape=[jax.ShapeDtypeStruct((2 * rows, wide), jnp.float32)] * 2,
        in_specs=[pl.BlockSpec(memory_space=pltpu.SMEM)] + [hbm] * len(operands) + [vmem] * len(before),
        out_specs=[vmem] * 2,
        scratch_shapes=[
            pltpu.VMEM((2, 2, 8, rows, 256), jnp.bfloat16),
            pltpu.VMEM((4 * rows, depth), jnp.bfloat16),
            pltpu.VMEM((depth, wide), jnp.bfloat16),
            pltpu.SemaphoreType.DMA((2,)),
            pltpu.SemaphoreType.DMA((12,)),
        ],
        compiler_params=pltpu.CompilerParams(vmem_limit_bytes=48 << 20),
        cost_estimate=pl.CostEstimate(flops=8 * rows * depth * wide, bytes_accessed=16 << 20, transcendentals=0),
    )(place, *operands, *before)


def cut_kernel(place, gate, up, near, away, give_near, give_away):
    for zh in range(2):
        for q in range(2):

            @pl.when((place[1] == zh) & (place[6] == q))
            def _(zh=zh, q=q):
                for out, half, side_q in ((near, zh, q), (away, 1 - zh, q), (give_near, zh, 1 - q), (give_away, 1 - zh, 1 - q)):
                    base = half * 896
                    for t in range(3):
                        lo = base + side_q * 512 + t * TILE
                        out[:, 2 * t * TILE : (2 * t + 1) * TILE] = gate[:, lo : lo + TILE]
                        out[:, (2 * t + 1) * TILE : (2 * t + 2) * TILE] = up[:, lo : lo + TILE]
                    lo = base + 384 + side_q * 64
                    out[:, 6 * TILE :] = jnp.concatenate([gate[:, lo : lo + 64], up[:, lo : lo + 64]], 1)


def cut(place, gate, up):
    vmem = pl.BlockSpec(memory_space=pltpu.VMEM)
    depth, wide = gate.shape[0], gate.shape[1] // 2
    return pl.pallas_call(
        cut_kernel,
        out_shape=[jax.ShapeDtypeStruct((depth, wide), gate.dtype)] * 4,
        in_specs=[pl.BlockSpec(memory_space=pltpu.SMEM), vmem, vmem],
        out_specs=[vmem] * 4,
        compiler_params=pltpu.CompilerParams(vmem_limit_bytes=24 << 20),
        cost_estimate=pl.CostEstimate(flops=0, bytes_accessed=4 << 20, transcendentals=0),
    )(place, gate, up)


def gated_kernel(place, kept, received, *outs):
    zh = place[1]
    rows, whole = outs[0].shape[0], kept.shape[1] // (2 * TILE)
    for n, out in enumerate(outs):
        at = pl.ds(pl.multiple_of(lax.rem(zh + n, 2) * rows, rows), rows)
        total = kept[at, :] + received[at, :]
        for t in range(whole):
            gate, up = total[:, 2 * t * TILE : (2 * t + 1) * TILE], total[:, (2 * t + 1) * TILE : (2 * t + 2) * TILE]
            out[:, t * TILE : (t + 1) * TILE] = (jax.nn.silu(gate) * up).astype(jnp.bfloat16)
        last = total[:, 2 * whole * TILE :]
        up = pltpu.roll(last, TILE // 2, 1)
        out[:, whole * TILE :] = (jax.nn.silu(last) * up).astype(jnp.bfloat16)[:, : TILE // 2]


def gated(place, kept, received):
    rows, wide = kept.shape
    vmem = pl.BlockSpec(memory_space=pltpu.VMEM)
    return pl.pallas_call(
        gated_kernel,
        out_shape=[jax.ShapeDtypeStruct((rows // 2, wide // 2), jnp.bfloat16)] * 2,
        in_specs=[pl.BlockSpec(memory_space=pltpu.SMEM), vmem, vmem],
        out_specs=[vmem] * 2,
        compiler_params=pltpu.CompilerParams(vmem_limit_bytes=16 << 20),
        cost_estimate=pl.CostEstimate(flops=8 * rows * wide, bytes_accessed=4 << 20, transcendentals=rows * wide // 2),
    )(place, kept, received)


def gather_kernel(place, *refs):
    blocks, out = refs[:4], refs[4]
    for zh in range(2):
        for q in range(2):

            @pl.when((place[1] == zh) & (place[6] == q))
            def _(zh=zh, q=q):
                for other in range(2):
                    base = (zh ^ other) * 896
                    low, high = blocks[2 * q + other], blocks[2 * (1 - q) + other]
                    out[:, base : base + 384] = low[:, :384]
                    out[:, base + 384 : base + 512] = jnp.concatenate([low[:, 384:], high[:, 384:]], 1)
                    out[:, base + 512 : base + 896] = high[:, :384]


def gather(place, blocks):
    vmem = pl.BlockSpec(memory_space=pltpu.VMEM)
    return pl.pallas_call(
        gather_kernel,
        out_shape=jax.ShapeDtypeStruct((blocks[0].shape[0], 1792), jnp.bfloat16),
        in_specs=[pl.BlockSpec(memory_space=pltpu.SMEM)] + [vmem] * 4,
        out_specs=vmem,
        compiler_params=pltpu.CompilerParams(vmem_limit_bytes=16 << 20),
        cost_estimate=pl.CostEstimate(flops=0, bytes_accessed=2 << 20, transcendentals=0),
    )(place, *blocks)


def along_y(value, d):
    return move(value, lambda x, y, z, c: (x, y - d, z, c))


def after(value, *others):
    return lax.optimization_barrier((value, *others))[0]


def per_device(tokens, gate_weight, up_weight):
    y, zh, x, zl, c = (lax.axis_index(a) for a in AXES)
    ahead = side(x, c)
    partner, summer = (x + ahead + 4) % 4, (x - ahead + 4) % 4
    over = (summer - ahead + 4) % 4
    q = ((x + 1 - c) // 2) % 2
    rows = tokens.shape[0] // NX

    def places(a, b):
        return jnp.stack([y, zh, zl, c, a, b, q]).astype(jnp.int32)

    send_place, keep_place = places(summer, over), places(x, partner)

    panel = lax.all_gather(tokens, ("zh", "zl", "c"), axis=0)
    near, away, give_near, give_away = cut(keep_place, gate_weight, up_weight)
    got_near, got_away = move(give_near, to_partner), move(give_away, to_partner)
    near = jnp.stack([near, got_near])
    near = [near, along_y(near, 1), near, along_y(near, 3)]

    panel = after(panel, got_away, near[1], near[3])
    away, got_away, near[2], panel = lax.optimization_barrier((away, got_away, near[2], panel))
    own, shared = (p.reshape(2, 8, NX, rows, 256) for p in (panel, move(panel, to_partner)))
    far = [jnp.stack([away[:, lo:hi], got_away[:, lo:hi]]) for lo, hi in PARTS]
    far[0] = move(far[0], to_antipode)
    near[2] = along_y(near[2], 2)
    far[1] = move(after(far[1], far[0], near[2]), to_antipode)
    far = [[f] + [along_y(f, d) for d in range(1, 4)] for f in far]

    sent = product(1, send_place, shared, near, far, product(0, send_place, own, near, far))
    sums = [move(sent[0], to_summer), move(sent[1], to_summer)]
    turn = after(keep_place, *sent)
    kept = product(1, turn, shared, near, far, product(0, turn, own, near, far))
    mine, over_z = gated(keep_place, kept[0], sums[0])
    over_x, over_both = gated(keep_place, kept[1], sums[1])
    blocks = [mine, move(over_z, to_antipode), move(over_x, to_partner), move(over_both, to_both)]
    return gather(keep_place, blocks)


def solution(mesh):
    fine = Mesh(np.array(mesh.devices).reshape(NY, 2, NX, NZ // 2, NC), AXES)
    rows, cols = ("y", "zh"), ("zl", "c")
    return jax.shard_map(
        per_device,
        mesh=fine,
        in_specs=(P(rows, ("x", *cols)), P(("x", *rows), cols), P(("x", *rows), cols)),
        out_specs=P((*rows, "x"), cols),
        check_vma=False,
    )
```

```python
import functools

import jax
import jax.numpy as jnp
import numpy as np
from jax import lax
from jax.experimental import pallas as pl
from jax.experimental.pallas import tpu as pltpu
from jax.sharding import Mesh
from jax.sharding import PartitionSpec as P

NX, NY, NZ, NC = 4, 4, 8, 2
AXES = ("y", "zh", "x", "zl", "c")
TILE = 128


def device_index(x, y, z, c):
    return ((y * 2 + z // 4) * NX + x) * 8 + (z % 4) * 2 + c


def side(x, c):
    return 1 - 2 * ((x + c) % 2)


def move(value, target):
    pairs = []
    for x in range(NX):
        for y in range(NY):
            for z in range(NZ):
                for c in range(NC):
                    tx, ty, tz, tc = target(x, y, z, c)
                    pairs.append((device_index(x, y, z, c), device_index(tx % NX, ty % NY, tz % NZ, tc)))
    return lax.ppermute(value, AXES, pairs)


def to_partner(x, y, z, c):
    return x + side(x, c), y, z, c


def to_crossed(x, y, z, c):
    return x + side(x, 1 - c), y, z, 1 - c


def to_antipode(x, y, z, c):
    return x, y, z + 4, c


def to_both(x, y, z, c):
    return x + side(x, c), y, z + 4, c


def to_summer(x, y, z, c):
    return x - side(x, c), y, z, c


def product_kernel(u, slots, place, panel, *refs):
    near, far, refs = refs[:4], refs[4:8], refs[8:]
    before, refs = refs[: u * len(slots)], refs[u * len(slots) :]
    outs, (pieces, lhs, rhs, lhs_sem, rhs_sem) = refs[: len(slots)], refs[len(slots) :]
    y, zh = place[0], place[1]
    rows, wide = pieces.shape[3], rhs.shape[1]
    tokens = [pltpu.make_async_copy(panel.at[:, :, place[slot]], pieces.at[i], lhs_sem.at[i]) for i, slot in enumerate(slots)]
    weights = []
    for d in range(4):
        k = lax.rem(y + d, 4) * 2
        for source, at in ((near[d].at[u], k + zh), (far[d], k + 1 - zh)):
            target = rhs.at[pl.ds(pl.multiple_of(at * 256, 256), 256)]
            weights.append(pltpu.make_async_copy(source, target, rhs_sem.at[len(weights)]))
    for copy in (*tokens, *weights):
        copy.start()
    for i in range(len(slots)):
        tokens[i].wait()
        for b in range(2):
            at = (i * 2 + b) * rows
            for k in range(8):
                lhs[at : at + rows, k * 256 : (k + 1) * 256] = pieces[i, b, k]
    for copy in weights:
        copy.wait()
    for lo in range(0, wide, 256):
        hi = min(lo + 256, wide)
        part = jnp.dot(lhs[...], rhs[:, lo:hi], preferred_element_type=jnp.float32)
        for i, out in enumerate(outs):
            mine = part[i * 2 * rows : (i + 1) * 2 * rows]
            out[:, lo:hi] = before[i][:, lo:hi] + mine if u else mine


def product(u, slots, place, panel, near, far, before=()):
    rows, depth, wide, n = panel.shape[3], 2048, far[u][0].shape[1], len(slots)
    hbm, vmem = pl.BlockSpec(memory_space=pltpu.HBM), pl.BlockSpec(memory_space=pltpu.VMEM)
    operands = [panel, *near, *far[u]]
    return pl.pallas_call(
        functools.partial(product_kernel, u, slots),
        out_shape=[jax.ShapeDtypeStruct((2 * rows, wide), jnp.float32)] * n,
        in_specs=[pl.BlockSpec(memory_space=pltpu.SMEM)] + [hbm] * len(operands) + [vmem] * len(before),
        out_specs=[vmem] * n,
        scratch_shapes=[
            pltpu.VMEM((n, 2, 8, rows, 256), jnp.bfloat16),
            pltpu.VMEM((2 * n * rows, depth), jnp.bfloat16),
            pltpu.VMEM((depth, wide), jnp.bfloat16),
            pltpu.SemaphoreType.DMA((n,)),
            pltpu.SemaphoreType.DMA((8,)),
        ],
        compiler_params=pltpu.CompilerParams(vmem_limit_bytes=60 << 20),
        cost_estimate=pl.CostEstimate(flops=4 * n * rows * depth * wide, bytes_accessed=8 * n << 20, transcendentals=0),
    )(place, *operands, *before)


def cut_kernel(place, gate, up, near, away, give_near, give_away):
    for zh in range(2):
        for q in range(2):

            @pl.when((place[1] == zh) & (place[6] == q))
            def _(zh=zh, q=q):
                for out, half, side_q in ((near, zh, q), (away, 1 - zh, q), (give_near, zh, 1 - q), (give_away, 1 - zh, 1 - q)):
                    base = half * 896
                    for t in range(3):
                        lo = base + side_q * 512 + t * TILE
                        out[:, 2 * t * TILE : (2 * t + 1) * TILE] = gate[:, lo : lo + TILE]
                        out[:, (2 * t + 1) * TILE : (2 * t + 2) * TILE] = up[:, lo : lo + TILE]
                    lo = base + 384 + side_q * 64
                    out[:, 6 * TILE :] = jnp.concatenate([gate[:, lo : lo + 64], up[:, lo : lo + 64]], 1)


def cut(place, gate, up):
    vmem = pl.BlockSpec(memory_space=pltpu.VMEM)
    depth, wide = gate.shape[0], gate.shape[1] // 2
    return pl.pallas_call(
        cut_kernel,
        out_shape=[jax.ShapeDtypeStruct((depth, wide), gate.dtype)] * 4,
        in_specs=[pl.BlockSpec(memory_space=pltpu.SMEM), vmem, vmem],
        out_specs=[vmem] * 4,
        compiler_params=pltpu.CompilerParams(vmem_limit_bytes=24 << 20),
        cost_estimate=pl.CostEstimate(flops=0, bytes_accessed=4 << 20, transcendentals=0),
    )(place, gate, up)


def gated_kernel(place, kept, received, *outs):
    zh = place[1]
    rows, whole = outs[0].shape[0], kept.shape[1] // (2 * TILE)
    for n, out in enumerate(outs):
        at = pl.ds(pl.multiple_of(lax.rem(zh + n, 2) * rows, rows), rows)
        total = kept[at, :] + received[at, :]
        for t in range(whole):
            gate, up = total[:, 2 * t * TILE : (2 * t + 1) * TILE], total[:, (2 * t + 1) * TILE : (2 * t + 2) * TILE]
            out[:, t * TILE : (t + 1) * TILE] = (jax.nn.silu(gate) * up).astype(jnp.bfloat16)
        last = total[:, 2 * whole * TILE :]
        up = pltpu.roll(last, TILE // 2, 1)
        out[:, whole * TILE :] = (jax.nn.silu(last) * up).astype(jnp.bfloat16)[:, : TILE // 2]


def gated(place, kept, received):
    rows, wide = kept.shape
    vmem = pl.BlockSpec(memory_space=pltpu.VMEM)
    return pl.pallas_call(
        gated_kernel,
        out_shape=[jax.ShapeDtypeStruct((rows // 2, wide // 2), jnp.bfloat16)] * 2,
        in_specs=[pl.BlockSpec(memory_space=pltpu.SMEM), vmem, vmem],
        out_specs=[vmem] * 2,
        compiler_params=pltpu.CompilerParams(vmem_limit_bytes=16 << 20),
        cost_estimate=pl.CostEstimate(flops=8 * rows * wide, bytes_accessed=4 << 20, transcendentals=rows * wide // 2),
    )(place, kept, received)


def gather_kernel(place, *refs):
    blocks, out = refs[:4], refs[4]
    for zh in range(2):
        for q in range(2):

            @pl.when((place[1] == zh) & (place[6] == q))
            def _(zh=zh, q=q):
                for other in range(2):
                    base = (zh ^ other) * 896
                    low, high = blocks[2 * q + other], blocks[2 * (1 - q) + other]
                    out[:, base : base + 384] = low[:, :384]
                    out[:, base + 384 : base + 512] = jnp.concatenate([low[:, 384:], high[:, 384:]], 1)
                    out[:, base + 512 : base + 896] = high[:, :384]


def gather(place, blocks):
    vmem = pl.BlockSpec(memory_space=pltpu.VMEM)
    return pl.pallas_call(
        gather_kernel,
        out_shape=jax.ShapeDtypeStruct((blocks[0].shape[0], 1792), jnp.bfloat16),
        in_specs=[pl.BlockSpec(memory_space=pltpu.SMEM)] + [vmem] * 4,
        out_specs=vmem,
        compiler_params=pltpu.CompilerParams(vmem_limit_bytes=16 << 20),
        cost_estimate=pl.CostEstimate(flops=0, bytes_accessed=2 << 20, transcendentals=0),
    )(place, *blocks)


def along_y(value, d):
    return move(value, lambda x, y, z, c: (x, y - d, z, c))


def after(value, *others):
    return lax.optimization_barrier((value, *others))[0]


def per_device(tokens, gate_weight, up_weight):
    y, zh, x, zl, c = (lax.axis_index(a) for a in AXES)
    ahead = side(x, c)
    partner, summer = (x + ahead + 4) % 4, (x - ahead + 4) % 4
    over = (summer - ahead + 4) % 4
    q = ((x + 1 - c) // 2) % 2
    rows = tokens.shape[0] // NX

    def places(a, b):
        return jnp.stack([y, zh, zl, c, a, b, q]).astype(jnp.int32)

    send_place, keep_place = places(summer, over), places(x, partner)

    panel = lax.all_gather(tokens, ("zh", "zl", "c"), axis=0)
    near, away, give_near, give_away = cut(keep_place, gate_weight, up_weight)
    got_near, got_away = move(give_near, to_partner), move(give_away, to_partner)
    near = jnp.stack([near, got_near])
    near = [near, along_y(near, 1), near, along_y(near, 3)]

    panel = after(panel, got_away, near[1], near[3])
    away, got_away, near[2], panel = lax.optimization_barrier((away, got_away, near[2], panel))
    own, shared = (p.reshape(2, 8, NX, rows, 256) for p in (panel, move(panel, to_partner)))
    far = [move(away, to_antipode)]
    near[2] = along_y(near[2], 2)
    far.append(move(after(got_away, far[0], near[2]), to_antipode))
    far = [[f] + [along_y(f, d) for d in range(1, 4)] for f in far]

    sent = product(0, (4, 5), send_place, own, near, far)
    kept = product(0, (4, 5), after(keep_place, *sent), own, near, far)
    sums, turn = [None, None], send_place
    for i in (1, 0):
        total = product(1, (4 + i,), turn, shared, near, far, sent[i : i + 1])[0]
        turn, sums[i] = after(send_place, total), move(total, to_summer)
    turn = after(keep_place, total)
    total = product(1, (5,), turn, shared, near, far, kept[1:])[0]
    over_x, over_both = gated(keep_place, total, sums[1])
    total = product(1, (4,), after(keep_place, over_x), shared, near, far, kept[:1])[0]
    over_x, over_both = move(over_x, to_partner), move(over_both, to_both)
    mine, over_z = gated(keep_place, total, after(sums[0], over_x, over_both))
    blocks = [mine, move(over_z, to_antipode), over_x, over_both]
    return gather(keep_place, blocks)


def solution(mesh):
    fine = Mesh(np.array(mesh.devices).reshape(NY, 2, NX, NZ // 2, NC), AXES)
    rows, cols = ("y", "zh"), ("zl", "c")
    return jax.shard_map(
        per_device,
        mesh=fine,
        in_specs=(P(rows, ("x", *cols)), P(("x", *rows), cols), P(("x", *rows), cols)),
        out_specs=P((*rows, "x"), cols),
        check_vma=False,
    )
```

```python
import functools

import jax
import jax.numpy as jnp
import numpy as np
from jax import lax
from jax.experimental import pallas as pl
from jax.experimental.pallas import tpu as pltpu
from jax.sharding import Mesh
from jax.sharding import PartitionSpec as P

NX, NY, NZ, NC = 4, 4, 8, 2
AXES = ("y", "zh", "x", "zl", "c")
TILE = 128
STEPS = ((0,), (1, 7), (2, 6), (3, 5), (4,))


def device_index(x, y, z, c):
    return ((y * 2 + z // 4) * NX + x) * 8 + (z % 4) * 2 + c


def side(x, c):
    return 1 - 2 * ((x + c) % 2)


def move(value, target):
    pairs = []
    for x in range(NX):
        for y in range(NY):
            for z in range(NZ):
                for c in range(NC):
                    tx, ty, tz, tc = target(x, y, z, c)
                    pairs.append((device_index(x, y, z, c), device_index(tx % NX, ty % NY, tz % NZ, tc)))
    return lax.ppermute(value, AXES, pairs)


def to_partner(x, y, z, c):
    return x + side(x, c), y, z, c


def to_crossed(x, y, z, c):
    return x + side(x, 1 - c), y, z, 1 - c


def to_antipode(x, y, z, c):
    return x, y, z + 4, c


def to_both(x, y, z, c):
    return x + side(x, c), y, z + 4, c


def to_summer(x, y, z, c):
    return x - side(x, c), y, z, c


def product_kernel(u, slots, place, *refs):
    tokens, near, far, refs = refs[:5], refs[5:9], refs[9:13], refs[13:]
    before, refs = refs[: u * len(slots)], refs[u * len(slots) :]
    outs, (pieces, lhs, rhs, lhs_sem, rhs_sem) = refs[: len(slots)], refs[len(slots) :]
    y, zh, zl, c = place[0], place[1], place[2], place[3]
    rows, wide = pieces.shape[3], rhs.shape[1]
    shares = []
    for i, slot in enumerate(slots):
        copies = []
        for blocks, offsets in zip(tokens, STEPS):
            for j, d in enumerate(offsets):
                z = lax.rem(zh * 4 + zl + d, 8)
                for e in range(2):
                    target = pieces.at[i, z // 4, lax.rem(z, 4) * 2 + lax.rem(c + e, 2)]
                    source = blocks.at[e * len(offsets) + j, place[slot]]
                    copies.append(pltpu.make_async_copy(source, target, lhs_sem.at[i * 16 + len(copies)]))
        shares.append(copies)
    weights = []
    for d in range(4):
        k = lax.rem(y + d + d % 2 * 2 * c, 4) * 2
        for source, at in ((near[d].at[u], k + zh), (far[d], k + 1 - zh)):
            target = rhs.at[pl.ds(pl.multiple_of(at * 256, 256), 256)]
            weights.append(pltpu.make_async_copy(source, target, rhs_sem.at[len(weights)]))
    for copies in (*shares, weights):
        for copy in copies:
            copy.start()
    for i in range(len(slots)):
        for copy in shares[i]:
            copy.wait()
        for b in range(2):
            at = (i * 2 + b) * rows
            for k in range(8):
                lhs[at : at + rows, k * 256 : (k + 1) * 256] = pieces[i, b, k]
    for copy in weights:
        copy.wait()
    for lo in range(0, wide, 256):
        hi = min(lo + 256, wide)
        part = jnp.dot(lhs[...], rhs[:, lo:hi], preferred_element_type=jnp.float32)
        for i, out in enumerate(outs):
            mine = part[i * 2 * rows : (i + 1) * 2 * rows]
            out[:, lo:hi] = before[i][:, lo:hi] + mine if u else mine


def product(u, slots, place, tokens, near, far, before=()):
    rows, depth, wide, n = tokens[0].shape[2], 2048, far[u][0].shape[1], len(slots)
    hbm, vmem = pl.BlockSpec(memory_space=pltpu.HBM), pl.BlockSpec(memory_space=pltpu.VMEM)
    operands = [*tokens, *near, *far[u]]
    return pl.pallas_call(
        functools.partial(product_kernel, u, slots),
        out_shape=[jax.ShapeDtypeStruct((2 * rows, wide), jnp.float32)] * n,
        in_specs=[pl.BlockSpec(memory_space=pltpu.SMEM)] + [hbm] * len(operands) + [vmem] * len(before),
        out_specs=[vmem] * n,
        scratch_shapes=[
            pltpu.VMEM((n, 2, 8, rows, 256), jnp.bfloat16),
            pltpu.VMEM((2 * n * rows, depth), jnp.bfloat16),
            pltpu.VMEM((depth, wide), jnp.bfloat16),
            pltpu.SemaphoreType.DMA((16 * n,)),
            pltpu.SemaphoreType.DMA((8,)),
        ],
        compiler_params=pltpu.CompilerParams(vmem_limit_bytes=60 << 20),
        cost_estimate=pl.CostEstimate(flops=4 * n * rows * depth * wide, bytes_accessed=8 * n << 20, transcendentals=0),
    )(place, *operands, *before)


def cut_kernel(place, gate, up, near, away, give_near, give_away):
    for zh in range(2):
        for q in range(2):

            @pl.when((place[1] == zh) & (place[6] == q))
            def _(zh=zh, q=q):
                for out, half, side_q in ((near, zh, q), (away, 1 - zh, q), (give_near, zh, 1 - q), (give_away, 1 - zh, 1 - q)):
                    base = half * 896
                    for t in range(3):
                        lo = base + side_q * 512 + t * TILE
                        out[:, 2 * t * TILE : (2 * t + 1) * TILE] = gate[:, lo : lo + TILE]
                        out[:, (2 * t + 1) * TILE : (2 * t + 2) * TILE] = up[:, lo : lo + TILE]
                    lo = base + 384 + side_q * 64
                    out[:, 6 * TILE :] = jnp.concatenate([gate[:, lo : lo + 64], up[:, lo : lo + 64]], 1)


def cut(place, gate, up):
    vmem = pl.BlockSpec(memory_space=pltpu.VMEM)
    depth, wide = gate.shape[0], gate.shape[1] // 2
    return pl.pallas_call(
        cut_kernel,
        out_shape=[jax.ShapeDtypeStruct((depth, wide), gate.dtype)] * 4,
        in_specs=[pl.BlockSpec(memory_space=pltpu.SMEM), vmem, vmem],
        out_specs=[vmem] * 4,
        compiler_params=pltpu.CompilerParams(vmem_limit_bytes=24 << 20),
        cost_estimate=pl.CostEstimate(flops=0, bytes_accessed=4 << 20, transcendentals=0),
    )(place, gate, up)


def gated_kernel(place, kept, received, *outs):
    zh = place[1]
    rows, whole = outs[0].shape[0], kept.shape[1] // (2 * TILE)
    for n, out in enumerate(outs):
        at = pl.ds(pl.multiple_of(lax.rem(zh + n, 2) * rows, rows), rows)
        total = kept[at, :] + received[at, :]
        for t in range(whole):
            gate, up = total[:, 2 * t * TILE : (2 * t + 1) * TILE], total[:, (2 * t + 1) * TILE : (2 * t + 2) * TILE]
            out[:, t * TILE : (t + 1) * TILE] = (jax.nn.silu(gate) * up).astype(jnp.bfloat16)
        last = total[:, 2 * whole * TILE :]
        up = pltpu.roll(last, TILE // 2, 1)
        out[:, whole * TILE :] = (jax.nn.silu(last) * up).astype(jnp.bfloat16)[:, : TILE // 2]


def gated(place, kept, received):
    rows, wide = kept.shape
    vmem = pl.BlockSpec(memory_space=pltpu.VMEM)
    return pl.pallas_call(
        gated_kernel,
        out_shape=[jax.ShapeDtypeStruct((rows // 2, wide // 2), jnp.bfloat16)] * 2,
        in_specs=[pl.BlockSpec(memory_space=pltpu.SMEM), vmem, vmem],
        out_specs=[vmem] * 2,
        compiler_params=pltpu.CompilerParams(vmem_limit_bytes=16 << 20),
        cost_estimate=pl.CostEstimate(flops=8 * rows * wide, bytes_accessed=4 << 20, transcendentals=rows * wide // 2),
    )(place, kept, received)


def gather_kernel(place, *refs):
    blocks, out = refs[:4], refs[4]
    for zh in range(2):
        for q in range(2):

            @pl.when((place[1] == zh) & (place[6] == q))
            def _(zh=zh, q=q):
                for other in range(2):
                    base = (zh ^ other) * 896
                    low, high = blocks[2 * q + other], blocks[2 * (1 - q) + other]
                    out[:, base : base + 384] = low[:, :384]
                    out[:, base + 384 : base + 512] = jnp.concatenate([low[:, 384:], high[:, 384:]], 1)
                    out[:, base + 512 : base + 896] = high[:, :384]


def gather(place, blocks):
    vmem = pl.BlockSpec(memory_space=pltpu.VMEM)
    return pl.pallas_call(
        gather_kernel,
        out_shape=jax.ShapeDtypeStruct((blocks[0].shape[0], 1792), jnp.bfloat16),
        in_specs=[pl.BlockSpec(memory_space=pltpu.SMEM)] + [vmem] * 4,
        out_specs=vmem,
        compiler_params=pltpu.CompilerParams(vmem_limit_bytes=16 << 20),
        cost_estimate=pl.CostEstimate(flops=0, bytes_accessed=2 << 20, transcendentals=0),
    )(place, *blocks)


def along_y(value, d):
    return move(value, lambda x, y, z, c: (x, y - d - d % 2 * 2 * c, z, c))


def after(value, *others):
    return lax.optimization_barrier((value, *others))[0]


def per_device(tokens, gate_weight, up_weight):
    y, zh, x, zl, c = (lax.axis_index(a) for a in AXES)
    ahead = side(x, c)
    partner, summer = (x + ahead + 4) % 4, (x - ahead + 4) % 4
    over = (summer - ahead + 4) % 4
    q = ((x + 1 - c) // 2) % 2
    rows = tokens.shape[0] // NX

    def places(a, b):
        return jnp.stack([y, zh, zl, c, a, b, q]).astype(jnp.int32)

    send_place, keep_place = places(summer, over), places(x, partner)

    block = behind = before = tokens.reshape(1, NX, rows, 256)
    steps = []
    for s in range(5):
        if s in (1, 2, 3):
            behind = move(behind, lambda x, y, z, c: (x, y, z - 1, c))
            before = move(before, lambda x, y, z, c: (x, y, z + 1, c))
            block = jnp.concatenate([behind, before])
        elif s == 4:
            block = move(jnp.where(c == 0, before, behind), lambda x, y, z, c: (x, y, z + 1 - 2 * c, c))
        steps.append(block)

    near, away, give_near, give_away = cut(keep_place, gate_weight, up_weight)
    got_near, got_away = move(give_near, to_partner), move(give_away, to_partner)
    near = [jnp.stack([near, got_near])]
    for d in (1, 3, 2):
        near.append(along_y(after(near[0], near[-1]), d))
    far = [move(after(away, steps[3]), to_antipode)]
    far.append(move(after(got_away, far[0]), to_antipode))

    own, shared = [], []
    waits = ((), (), near[1:2], near[2:3], (near[3], far[0]))
    for s in range(5):
        own.append(jnp.concatenate([steps[s], move(steps[s], lambda x, y, z, c: (x, y, z, 1 - c))]))
        shared.append(move(after(own[s], *shared[-1:], *waits[s]), to_partner))
    near = [near[0], near[1], near[3], near[2]]
    far = [[f] + [along_y(f, d) for d in range(1, 4)] for f in far]

    sent = product(0, (4, 5), send_place, own, near, far)
    kept = product(0, (4, 5), after(keep_place, *sent), own, near, far)
    sums, turn = [None, None], send_place
    for i in (1, 0):
        total = product(1, (4 + i,), turn, shared, near, far, sent[i : i + 1])[0]
        turn, sums[i] = after(send_place, total), move(total, to_summer)
    turn = after(keep_place, total)
    total = product(1, (5,), turn, shared, near, far, kept[1:])[0]
    over_x, over_both = gated(keep_place, total, sums[1])
    total = product(1, (4,), after(keep_place, over_x), shared, near, far, kept[:1])[0]
    over_x, over_both = move(over_x, to_partner), move(over_both, to_both)
    mine, over_z = gated(keep_place, total, after(sums[0], over_x, over_both))
    blocks = [mine, move(over_z, to_antipode), over_x, over_both]
    return gather(keep_place, blocks)


def solution(mesh):
    fine = Mesh(np.array(mesh.devices).reshape(NY, 2, NX, NZ // 2, NC), AXES)
    rows, cols = ("y", "zh"), ("zl", "c")
    return jax.shard_map(
        per_device,
        mesh=fine,
        in_specs=(P(rows, ("x", *cols)), P(("x", *rows), cols), P(("x", *rows), cols)),
        out_specs=P((*rows, "x"), cols),
        check_vma=False,
    )
```

```python
import functools

import jax
import jax.numpy as jnp
import numpy as np
from jax import lax
from jax.experimental import pallas as pl
from jax.experimental.pallas import tpu as pltpu
from jax.sharding import Mesh
from jax.sharding import PartitionSpec as P

NX, NY, NZ, NC = 4, 4, 8, 2
AXES = ("y", "zh", "x", "zl", "c")
TILE = 128


def device_index(x, y, z, c):
    return ((y * 2 + z // 4) * NX + x) * 8 + (z % 4) * 2 + c


def side(x, c):
    return 1 - 2 * ((x + c) % 2)


def move(value, target):
    pairs = []
    for x in range(NX):
        for y in range(NY):
            for z in range(NZ):
                for c in range(NC):
                    tx, ty, tz, tc = target(x, y, z, c)
                    pairs.append((device_index(x, y, z, c), device_index(tx % NX, ty % NY, tz % NZ, tc)))
    return lax.ppermute(value, AXES, pairs)


def to_partner(x, y, z, c):
    return x + side(x, c), y, z, c


def to_crossed(x, y, z, c):
    return x + side(x, 1 - c), y, z, 1 - c


def to_antipode(x, y, z, c):
    return x, y, z + 4, c


def to_both(x, y, z, c):
    return x + side(x, c), y, z + 4, c


def to_summer(x, y, z, c):
    return x - side(x, c), y, z, c


def product_kernel(u, halves, place, panel, *refs):
    near, far, refs = refs[:4], refs[4:8], refs[8:]
    n = len(halves)
    before, outs, (pieces, lhs, rhs, lhs_sem, rhs_sem) = refs[: u * n], refs[u * n : u * n + n], refs[u * n + n :]
    y, zh = place[0], place[1]
    rows, wide = pieces.shape[3], rhs.shape[1]
    tokens = []
    for i, half in enumerate(halves):
        for j in range(2):
            source = panel.at[lax.rem(zh + half, 2), :, place[4 + j]]
            tokens.append(pltpu.make_async_copy(source, pieces.at[i, j], lhs_sem.at[2 * i + j]))
    weights = []
    for d in range(4):
        k = lax.rem(y + d, 4) * 2
        for source, at in ((near[d].at[u], k + zh), (far[d], k + 1 - zh)):
            target = rhs.at[pl.ds(pl.multiple_of(at * 256, 256), 256)]
            weights.append(pltpu.make_async_copy(source, target, rhs_sem.at[len(weights)]))
    for copy in (*tokens, *weights):
        copy.start()
    for i in range(n):
        for j in range(2):
            tokens[2 * i + j].wait()
            at = (i * 2 + j) * rows
            for k in range(8):
                lhs[at : at + rows, k * 256 : (k + 1) * 256] = pieces[i, j, k]
    for copy in weights:
        copy.wait()
    for lo in range(0, wide, 256):
        hi = min(lo + 256, wide)
        part = jnp.dot(lhs[...], rhs[:, lo:hi], preferred_element_type=jnp.float32)
        for i, out in enumerate(outs):
            mine = part[i * 2 * rows : (i + 1) * 2 * rows]
            out[:, lo:hi] = before[i][:, lo:hi] + mine if u else mine


def product(u, halves, place, panel, near, far, before=()):
    rows, depth, wide, n = panel.shape[3], 2048, far[u][0].shape[1], len(halves)
    hbm, vmem = pl.BlockSpec(memory_space=pltpu.HBM), pl.BlockSpec(memory_space=pltpu.VMEM)
    operands = [panel, *near, *far[u]]
    return pl.pallas_call(
        functools.partial(product_kernel, u, halves),
        out_shape=[jax.ShapeDtypeStruct((2 * rows, wide), jnp.float32)] * n,
        in_specs=[pl.BlockSpec(memory_space=pltpu.SMEM)] + [hbm] * len(operands) + [vmem] * len(before),
        out_specs=[vmem] * n,
        scratch_shapes=[
            pltpu.VMEM((n, 2, 8, rows, 256), jnp.bfloat16),
            pltpu.VMEM((2 * n * rows, depth), jnp.bfloat16),
            pltpu.VMEM((depth, wide), jnp.bfloat16),
            pltpu.SemaphoreType.DMA((2 * n,)),
            pltpu.SemaphoreType.DMA((8,)),
        ],
        compiler_params=pltpu.CompilerParams(vmem_limit_bytes=60 << 20),
        cost_estimate=pl.CostEstimate(flops=4 * n * rows * depth * wide, bytes_accessed=8 * n << 20, transcendentals=0),
    )(place, *operands, *before)


def cut_kernel(place, gate, up, near, away, give_near, give_away):
    for zh in range(2):
        for q in range(2):

            @pl.when((place[1] == zh) & (place[6] == q))
            def _(zh=zh, q=q):
                for out, half, side_q in ((near, zh, q), (away, 1 - zh, q), (give_near, zh, 1 - q), (give_away, 1 - zh, 1 - q)):
                    base = half * 896
                    for t in range(3):
                        lo = base + side_q * 512 + t * TILE
                        out[:, 2 * t * TILE : (2 * t + 1) * TILE] = gate[:, lo : lo + TILE]
                        out[:, (2 * t + 1) * TILE : (2 * t + 2) * TILE] = up[:, lo : lo + TILE]
                    lo = base + 384 + side_q * 64
                    out[:, 6 * TILE :] = jnp.concatenate([gate[:, lo : lo + 64], up[:, lo : lo + 64]], 1)


def cut(place, gate, up):
    vmem = pl.BlockSpec(memory_space=pltpu.VMEM)
    depth, wide = gate.shape[0], gate.shape[1] // 2
    return pl.pallas_call(
        cut_kernel,
        out_shape=[jax.ShapeDtypeStruct((depth, wide), gate.dtype)] * 4,
        in_specs=[pl.BlockSpec(memory_space=pltpu.SMEM), vmem, vmem],
        out_specs=[vmem] * 4,
        compiler_params=pltpu.CompilerParams(vmem_limit_bytes=24 << 20),
        cost_estimate=pl.CostEstimate(flops=0, bytes_accessed=4 << 20, transcendentals=0),
    )(place, gate, up)


def gated_kernel(kept, received, *outs):
    rows, whole = outs[0].shape[0], kept.shape[1] // (2 * TILE)
    for n, out in enumerate(outs):
        at = slice(n * rows, (n + 1) * rows)
        total = kept[at, :] + received[at, :]
        for t in range(whole):
            gate, up = total[:, 2 * t * TILE : (2 * t + 1) * TILE], total[:, (2 * t + 1) * TILE : (2 * t + 2) * TILE]
            out[:, t * TILE : (t + 1) * TILE] = (jax.nn.silu(gate) * up).astype(jnp.bfloat16)
        last = total[:, 2 * whole * TILE :]
        up = pltpu.roll(last, TILE // 2, 1)
        out[:, whole * TILE :] = (jax.nn.silu(last) * up).astype(jnp.bfloat16)[:, : TILE // 2]


def gated(kept, received):
    rows, wide = kept.shape
    vmem = pl.BlockSpec(memory_space=pltpu.VMEM)
    return pl.pallas_call(
        gated_kernel,
        out_shape=[jax.ShapeDtypeStruct((rows // 2, wide // 2), jnp.bfloat16)] * 2,
        in_specs=[vmem, vmem],
        out_specs=[vmem] * 2,
        compiler_params=pltpu.CompilerParams(vmem_limit_bytes=16 << 20),
        cost_estimate=pl.CostEstimate(flops=8 * rows * wide, bytes_accessed=4 << 20, transcendentals=rows * wide // 2),
    )(kept, received)


def gather_kernel(place, *refs):
    blocks, out = refs[:4], refs[4]
    for zh in range(2):
        for q in range(2):

            @pl.when((place[1] == zh) & (place[6] == q))
            def _(zh=zh, q=q):
                for other in range(2):
                    base = (zh ^ other) * 896
                    low, high = blocks[2 * q + other], blocks[2 * (1 - q) + other]
                    out[:, base : base + 384] = low[:, :384]
                    out[:, base + 384 : base + 512] = jnp.concatenate([low[:, 384:], high[:, 384:]], 1)
                    out[:, base + 512 : base + 896] = high[:, :384]


def gather(place, blocks):
    vmem = pl.BlockSpec(memory_space=pltpu.VMEM)
    return pl.pallas_call(
        gather_kernel,
        out_shape=jax.ShapeDtypeStruct((blocks[0].shape[0], 1792), jnp.bfloat16),
        in_specs=[pl.BlockSpec(memory_space=pltpu.SMEM)] + [vmem] * 4,
        out_specs=vmem,
        compiler_params=pltpu.CompilerParams(vmem_limit_bytes=16 << 20),
        cost_estimate=pl.CostEstimate(flops=0, bytes_accessed=2 << 20, transcendentals=0),
    )(place, *blocks)


def along_y(value, d):
    return move(value, lambda x, y, z, c: (x, y - d, z, c))


def after(value, *others):
    return lax.optimization_barrier((value, *others))[0]


def per_device(tokens, gate_weight, up_weight):
    y, zh, x, zl, c = (lax.axis_index(a) for a in AXES)
    ahead = side(x, c)
    partner, summer = (x + ahead + 4) % 4, (x - ahead + 4) % 4
    over = (summer - ahead + 4) % 4
    q = ((x + 1 - c) // 2) % 2
    rows = tokens.shape[0] // NX

    def places(a, b):
        return jnp.stack([y, zh, zl, c, a, b, q]).astype(jnp.int32)

    send_place, keep_place = places(summer, over), places(x, partner)

    panel = lax.all_gather(tokens, ("zh", "zl", "c"), axis=0)
    near, away, give_near, give_away = cut(keep_place, gate_weight, up_weight)
    got_near, got_away = move(give_near, to_partner), move(give_away, to_partner)
    near = jnp.stack([near, got_near])
    near = [near, along_y(near, 1), near, along_y(near, 3)]

    panel = after(panel, got_away, near[1], near[3])
    away, got_away, near[2], panel = lax.optimization_barrier((away, got_away, near[2], panel))
    own, shared = (p.reshape(2, 8, NX, rows, 256) for p in (panel, move(panel, to_partner)))
    far = [move(away, to_antipode)]
    near[2] = along_y(near[2], 2)
    far.append(move(after(got_away, far[0], near[2]), to_antipode))
    far = [[f] + [along_y(f, d) for d in range(1, 4)] for f in far]

    sent = product(0, (0, 1), send_place, own, near, far)
    kept = product(0, (0, 1), after(keep_place, *sent), own, near, far)
    sums, turn = [None, None], after(send_place, kept[0])
    for half in (1, 0):
        total = product(1, (half,), turn, shared, near, far, sent[half : half + 1])[0]
        turn, sums[half] = after(send_place, total), move(total, to_summer)
    total = product(1, (1,), after(keep_place, total), shared, near, far, kept[1:])[0]
    over_z, over_both = gated(total, sums[1])
    total = product(1, (0,), after(keep_place, over_z), shared, near, far, kept[:1])[0]
    over_z, over_both = move(over_z, to_antipode), move(over_both, to_both)
    mine, over_x = gated(total, after(sums[0], over_z, over_both))
    blocks = [mine, over_z, move(over_x, to_partner), over_both]
    return gather(keep_place, blocks)


def solution(mesh):
    fine = Mesh(np.array(mesh.devices).reshape(NY, 2, NX, NZ // 2, NC), AXES)
    rows, cols = ("y", "zh"), ("zl", "c")
    return jax.shard_map(
        per_device,
        mesh=fine,
        in_specs=(P(rows, ("x", *cols)), P(("x", *rows), cols), P(("x", *rows), cols)),
        out_specs=P((*rows, "x"), cols),
        check_vma=False,
    )
```

```python
import functools

import jax
import jax.numpy as jnp
import numpy as np
from jax import lax
from jax.experimental import pallas as pl
from jax.experimental.pallas import tpu as pltpu
from jax.sharding import Mesh
from jax.sharding import PartitionSpec as P

NX, NY, NZ, NC = 4, 4, 8, 2
AXES = ("y", "zh", "x", "zl", "c")
TILE = 128


def device_index(x, y, z, c):
    return ((y * 2 + z // 4) * NX + x) * 8 + (z % 4) * 2 + c


def side(x, c):
    return 1 - 2 * ((x + c) % 2)


def move(value, target):
    pairs = []
    for x in range(NX):
        for y in range(NY):
            for z in range(NZ):
                for c in range(NC):
                    tx, ty, tz, tc = target(x, y, z, c)
                    pairs.append((device_index(x, y, z, c), device_index(tx % NX, ty % NY, tz % NZ, tc)))
    return lax.ppermute(value, AXES, pairs)


def to_partner(x, y, z, c):
    return x + side(x, c), y, z, c


def to_crossed(x, y, z, c):
    return x + side(x, 1 - c), y, z, 1 - c


def to_antipode(x, y, z, c):
    return x, y, z + 4, c


def to_both(x, y, z, c):
    return x + side(x, c), y, z + 4, c


def to_summer(x, y, z, c):
    return x - side(x, c), y, z, c


def product_kernel(u, halves, place, panel, *refs):
    near, far, refs = refs[:4], refs[4:8], refs[8:]
    n = len(halves)
    before, outs, (pieces, lhs, rhs, lhs_sem, rhs_sem) = refs[: u * n], refs[u * n : u * n + n], refs[u * n + n :]
    y, zh = place[0], place[1]
    rows, wide = pieces.shape[3], rhs.shape[1]
    tokens = []
    for i, half in enumerate(halves):
        for j in range(2):
            source = panel.at[lax.rem(zh + half, 2), :, place[4 + j]]
            tokens.append(pltpu.make_async_copy(source, pieces.at[i, j], lhs_sem.at[2 * i + j]))
    weights = []
    for d in range(4):
        k = lax.rem(y + d + d % 2 * 2 * place[3], 4) * 2
        for source, at in ((near[d].at[u], k + zh), (far[d], k + 1 - zh)):
            target = rhs.at[pl.ds(pl.multiple_of(at * 256, 256), 256)]
            weights.append(pltpu.make_async_copy(source, target, rhs_sem.at[len(weights)]))
    for copy in (*tokens, *weights):
        copy.start()
    for i in range(n):
        for j in range(2):
            tokens[2 * i + j].wait()
            at = (i * 2 + j) * rows
            for k in range(8):
                lhs[at : at + rows, k * 256 : (k + 1) * 256] = pieces[i, j, k]
    for copy in weights:
        copy.wait()
    for lo in range(0, wide, 256):
        hi = min(lo + 256, wide)
        part = jnp.dot(lhs[...], rhs[:, lo:hi], preferred_element_type=jnp.float32)
        for i, out in enumerate(outs):
            mine = part[i * 2 * rows : (i + 1) * 2 * rows]
            out[:, lo:hi] = before[i][:, lo:hi] + mine if u else mine


def product(u, halves, place, panel, near, far, before=()):
    rows, depth, wide, n = panel.shape[3], 2048, far[u][0].shape[1], len(halves)
    hbm, vmem = pl.BlockSpec(memory_space=pltpu.HBM), pl.BlockSpec(memory_space=pltpu.VMEM)
    operands = [panel, *near, *far[u]]
    return pl.pallas_call(
        functools.partial(product_kernel, u, halves),
        out_shape=[jax.ShapeDtypeStruct((2 * rows, wide), jnp.float32)] * n,
        in_specs=[pl.BlockSpec(memory_space=pltpu.SMEM)] + [hbm] * len(operands) + [vmem] * len(before),
        out_specs=[vmem] * n,
        scratch_shapes=[
            pltpu.VMEM((n, 2, 8, rows, 256), jnp.bfloat16),
            pltpu.VMEM((2 * n * rows, depth), jnp.bfloat16),
            pltpu.VMEM((depth, wide), jnp.bfloat16),
            pltpu.SemaphoreType.DMA((2 * n,)),
            pltpu.SemaphoreType.DMA((8,)),
        ],
        compiler_params=pltpu.CompilerParams(vmem_limit_bytes=60 << 20),
        cost_estimate=pl.CostEstimate(flops=4 * n * rows * depth * wide, bytes_accessed=8 * n << 20, transcendentals=0),
    )(place, *operands, *before)


def cut_kernel(place, gate, up, near, away, give_near, give_away):
    for zh in range(2):
        for q in range(2):

            @pl.when((place[1] == zh) & (place[6] == q))
            def _(zh=zh, q=q):
                for out, half, side_q in ((near, zh, q), (away, 1 - zh, q), (give_near, zh, 1 - q), (give_away, 1 - zh, 1 - q)):
                    base = half * 896
                    for t in range(3):
                        lo = base + side_q * 512 + t * TILE
                        out[:, 2 * t * TILE : (2 * t + 1) * TILE] = gate[:, lo : lo + TILE]
                        out[:, (2 * t + 1) * TILE : (2 * t + 2) * TILE] = up[:, lo : lo + TILE]
                    lo = base + 384 + side_q * 64
                    out[:, 6 * TILE :] = jnp.concatenate([gate[:, lo : lo + 64], up[:, lo : lo + 64]], 1)


def cut(place, gate, up):
    vmem = pl.BlockSpec(memory_space=pltpu.VMEM)
    depth, wide = gate.shape[0], gate.shape[1] // 2
    return pl.pallas_call(
        cut_kernel,
        out_shape=[jax.ShapeDtypeStruct((depth, wide), gate.dtype)] * 4,
        in_specs=[pl.BlockSpec(memory_space=pltpu.SMEM), vmem, vmem],
        out_specs=[vmem] * 4,
        compiler_params=pltpu.CompilerParams(vmem_limit_bytes=24 << 20),
        cost_estimate=pl.CostEstimate(flops=0, bytes_accessed=4 << 20, transcendentals=0),
    )(place, gate, up)


def gated_kernel(kept, received, *outs):
    rows, whole = outs[0].shape[0], kept.shape[1] // (2 * TILE)
    for n, out in enumerate(outs):
        at = slice(n * rows, (n + 1) * rows)
        total = kept[at, :] + received[at, :]
        for t in range(whole):
            gate, up = total[:, 2 * t * TILE : (2 * t + 1) * TILE], total[:, (2 * t + 1) * TILE : (2 * t + 2) * TILE]
            out[:, t * TILE : (t + 1) * TILE] = (jax.nn.silu(gate) * up).astype(jnp.bfloat16)
        last = total[:, 2 * whole * TILE :]
        up = pltpu.roll(last, TILE // 2, 1)
        out[:, whole * TILE :] = (jax.nn.silu(last) * up).astype(jnp.bfloat16)[:, : TILE // 2]


def gated(kept, received):
    rows, wide = kept.shape
    vmem = pl.BlockSpec(memory_space=pltpu.VMEM)
    return pl.pallas_call(
        gated_kernel,
        out_shape=[jax.ShapeDtypeStruct((rows // 2, wide // 2), jnp.bfloat16)] * 2,
        in_specs=[vmem, vmem],
        out_specs=[vmem] * 2,
        compiler_params=pltpu.CompilerParams(vmem_limit_bytes=16 << 20),
        cost_estimate=pl.CostEstimate(flops=8 * rows * wide, bytes_accessed=4 << 20, transcendentals=rows * wide // 2),
    )(kept, received)


def gather_kernel(place, *refs):
    blocks, out = refs[:4], refs[4]
    for zh in range(2):
        for q in range(2):

            @pl.when((place[1] == zh) & (place[6] == q))
            def _(zh=zh, q=q):
                for other in range(2):
                    base = (zh ^ other) * 896
                    low, high = blocks[2 * q + other], blocks[2 * (1 - q) + other]
                    out[:, base : base + 384] = low[:, :384]
                    out[:, base + 384 : base + 512] = jnp.concatenate([low[:, 384:], high[:, 384:]], 1)
                    out[:, base + 512 : base + 896] = high[:, :384]


def gather(place, blocks):
    vmem = pl.BlockSpec(memory_space=pltpu.VMEM)
    return pl.pallas_call(
        gather_kernel,
        out_shape=jax.ShapeDtypeStruct((blocks[0].shape[0], 1792), jnp.bfloat16),
        in_specs=[pl.BlockSpec(memory_space=pltpu.SMEM)] + [vmem] * 4,
        out_specs=vmem,
        compiler_params=pltpu.CompilerParams(vmem_limit_bytes=16 << 20),
        cost_estimate=pl.CostEstimate(flops=0, bytes_accessed=2 << 20, transcendentals=0),
    )(place, *blocks)


def along_y(value, d):
    return move(value, lambda x, y, z, c: (x, y - d - 2 * c, z, c))


def after(value, *others):
    return lax.optimization_barrier((value, *others))[0]


def per_device(tokens, gate_weight, up_weight):
    y, zh, x, zl, c = (lax.axis_index(a) for a in AXES)
    ahead = side(x, c)
    partner, summer = (x + ahead + 4) % 4, (x - ahead + 4) % 4
    over = (summer - ahead + 4) % 4
    q = ((x + 1 - c) // 2) % 2
    rows = tokens.shape[0] // NX

    def places(a, b):
        return jnp.stack([y, zh, zl, c, a, b, q]).astype(jnp.int32)

    send_place, keep_place = places(summer, over), places(x, partner)

    panel = lax.all_gather(tokens, ("zh", "zl", "c"), axis=0)
    near, away, give_near, give_away = cut(keep_place, gate_weight, up_weight)
    got_near, got_away = move(give_near, to_partner), move(give_away, to_partner)
    near = jnp.stack([near, got_near])
    near = [near, along_y(near, 1), near, along_y(near, 3)]

    panel = after(panel, got_away, near[1], near[3])
    away, got_away, near[2], panel = lax.optimization_barrier((away, got_away, near[1], panel))
    own, shared = (p.reshape(2, 8, NX, rows, 256) for p in (panel, move(panel, to_partner)))
    far = [move(away, to_antipode)]
    near[2] = along_y(near[2], 1)
    far.append(move(after(got_away, far[0]), to_antipode))
    for u in range(2):
        block = after(far[u], *far[0][1:]) if u else far[u]
        one, three = along_y(block, 1), along_y(block, 3)
        far[u] = [block, one, along_y(one, 1), three]

    sent = product(0, (0, 1), send_place, own, near, far)
    kept = product(0, (0, 1), after(keep_place, *sent), own, near, far)
    sums, turn = [None, None], after(send_place, kept[0])
    for half in (1, 0):
        total = product(1, (half,), turn, shared, near, far, sent[half : half + 1])[0]
        turn, sums[half] = after(send_place, total), move(total, to_summer)
    total = product(1, (1,), after(keep_place, total), shared, near, far, kept[1:])[0]
    over_z, over_both = gated(total, sums[1])
    total = product(1, (0,), after(keep_place, over_z), shared, near, far, kept[:1])[0]
    over_z, over_both = move(over_z, to_antipode), move(over_both, to_both)
    mine, over_x = gated(total, after(sums[0], over_z, over_both))
    blocks = [mine, over_z, move(over_x, to_partner), over_both]
    return gather(keep_place, blocks)


def solution(mesh):
    fine = Mesh(np.array(mesh.devices).reshape(NY, 2, NX, NZ // 2, NC), AXES)
    rows, cols = ("y", "zh"), ("zl", "c")
    return jax.shard_map(
        per_device,
        mesh=fine,
        in_specs=(P(rows, ("x", *cols)), P(("x", *rows), cols), P(("x", *rows), cols)),
        out_specs=P((*rows, "x"), cols),
        check_vma=False,
    )
```

```python
import functools

import jax
import jax.numpy as jnp
import numpy as np
from jax import lax
from jax.experimental import pallas as pl
from jax.experimental.pallas import tpu as pltpu
from jax.sharding import Mesh
from jax.sharding import PartitionSpec as P

NX, NY, NZ, NC = 4, 4, 8, 2
AXES = ("y", "zh", "x", "zl", "c")
TILE = 128


def device_index(x, y, z, c):
    return ((y * 2 + z // 4) * NX + x) * 8 + (z % 4) * 2 + c


def side(x, c):
    return 1 - 2 * ((x + c) % 2)


def move(value, target):
    pairs = []
    for x in range(NX):
        for y in range(NY):
            for z in range(NZ):
                for c in range(NC):
                    tx, ty, tz, tc = target(x, y, z, c)
                    pairs.append((device_index(x, y, z, c), device_index(tx % NX, ty % NY, tz % NZ, tc)))
    return lax.ppermute(value, AXES, pairs)


def to_partner(x, y, z, c):
    return x + side(x, c), y, z, c


def to_crossed(x, y, z, c):
    return x + side(x, 1 - c), y, z, 1 - c


def to_antipode(x, y, z, c):
    return x, y, z + 4, c


def to_both(x, y, z, c):
    return x + side(x, c), y, z + 4, c


def to_summer(x, y, z, c):
    return x - side(x, c), y, z, c


def product_kernel(u, halves, place, panel, *refs):
    near, far, refs = refs[:4], refs[4:8], refs[8:]
    n = len(halves)
    before, outs, (pieces, lhs, rhs, lhs_sem, rhs_sem) = refs[: u * n], refs[u * n : u * n + n], refs[u * n + n :]
    y, zh = place[0], place[1]
    rows, wide = pieces.shape[3], rhs.shape[1]
    tokens = []
    for i, half in enumerate(halves):
        for j in range(2):
            source = panel.at[lax.rem(zh + half, 2), :, place[4 + j]]
            tokens.append(pltpu.make_async_copy(source, pieces.at[i, j], lhs_sem.at[2 * i + j]))
    weights = []
    for d in range(4):
        k = lax.rem(y + d + d % 2 * 2 * place[3], 4) * 2
        for source, at in ((near[d].at[u], k + zh), (far[d], k + 1 - zh)):
            target = rhs.at[pl.ds(pl.multiple_of(at * 256, 256), 256)]
            weights.append(pltpu.make_async_copy(source, target, rhs_sem.at[len(weights)]))
    for copy in (*tokens, *weights):
        copy.start()
    for i in range(n):
        for j in range(2):
            tokens[2 * i + j].wait()
            at = (i * 2 + j) * rows
            for k in range(8):
                lhs[at : at + rows, k * 256 : (k + 1) * 256] = pieces[i, j, k]
    for copy in weights:
        copy.wait()
    for lo in range(0, wide, 256):
        hi = min(lo + 256, wide)
        part = jnp.dot(lhs[...], rhs[:, lo:hi], preferred_element_type=jnp.float32)
        for i, out in enumerate(outs):
            mine = part[i * 2 * rows : (i + 1) * 2 * rows]
            out[:, lo:hi] = before[i][:, lo:hi] + mine if u else mine


def product(u, halves, place, panel, near, far, before=()):
    rows, depth, wide, n = panel.shape[3], 2048, far[u][0].shape[1], len(halves)
    hbm, vmem = pl.BlockSpec(memory_space=pltpu.HBM), pl.BlockSpec(memory_space=pltpu.VMEM)
    operands = [panel, *near, *far[u]]
    return pl.pallas_call(
        functools.partial(product_kernel, u, halves),
        out_shape=[jax.ShapeDtypeStruct((2 * rows, wide), jnp.float32)] * n,
        in_specs=[pl.BlockSpec(memory_space=pltpu.SMEM)] + [hbm] * len(operands) + [vmem] * len(before),
        out_specs=[vmem] * n,
        scratch_shapes=[
            pltpu.VMEM((n, 2, 8, rows, 256), jnp.bfloat16),
            pltpu.VMEM((2 * n * rows, depth), jnp.bfloat16),
            pltpu.VMEM((depth, wide), jnp.bfloat16),
            pltpu.SemaphoreType.DMA((2 * n,)),
            pltpu.SemaphoreType.DMA((8,)),
        ],
        compiler_params=pltpu.CompilerParams(vmem_limit_bytes=60 << 20),
        cost_estimate=pl.CostEstimate(flops=4 * n * rows * depth * wide, bytes_accessed=8 * n << 20, transcendentals=0),
    )(place, *operands, *before)


def cut_kernel(place, gate, up, near, away, give_near, give_away):
    for zh in range(2):
        for q in range(2):

            @pl.when((place[1] == zh) & (place[6] == q))
            def _(zh=zh, q=q):
                for out, half, side_q in ((near, zh, q), (away, 1 - zh, q), (give_near, zh, 1 - q), (give_away, 1 - zh, 1 - q)):
                    base = half * 896
                    for t in range(3):
                        lo = base + side_q * 512 + t * TILE
                        out[:, 2 * t * TILE : (2 * t + 1) * TILE] = gate[:, lo : lo + TILE]
                        out[:, (2 * t + 1) * TILE : (2 * t + 2) * TILE] = up[:, lo : lo + TILE]
                    lo = base + 384 + side_q * 64
                    out[:, 6 * TILE :] = jnp.concatenate([gate[:, lo : lo + 64], up[:, lo : lo + 64]], 1)


def cut(place, gate, up):
    vmem = pl.BlockSpec(memory_space=pltpu.VMEM)
    depth, wide = gate.shape[0], gate.shape[1] // 2
    return pl.pallas_call(
        cut_kernel,
        out_shape=[jax.ShapeDtypeStruct((depth, wide), gate.dtype)] * 4,
        in_specs=[pl.BlockSpec(memory_space=pltpu.SMEM), vmem, vmem],
        out_specs=[vmem] * 4,
        compiler_params=pltpu.CompilerParams(vmem_limit_bytes=24 << 20),
        cost_estimate=pl.CostEstimate(flops=0, bytes_accessed=4 << 20, transcendentals=0),
    )(place, gate, up)


def gated_kernel(kept, received, *outs):
    rows, whole = outs[0].shape[0], kept.shape[1] // (2 * TILE)
    for n, out in enumerate(outs):
        at = slice(n * rows, (n + 1) * rows)
        total = kept[at, :] + received[at, :]
        for t in range(whole):
            gate, up = total[:, 2 * t * TILE : (2 * t + 1) * TILE], total[:, (2 * t + 1) * TILE : (2 * t + 2) * TILE]
            out[:, t * TILE : (t + 1) * TILE] = (jax.nn.silu(gate) * up).astype(jnp.bfloat16)
        last = total[:, 2 * whole * TILE :]
        up = pltpu.roll(last, TILE // 2, 1)
        out[:, whole * TILE :] = (jax.nn.silu(last) * up).astype(jnp.bfloat16)[:, : TILE // 2]


def gated(kept, received):
    rows, wide = kept.shape
    vmem = pl.BlockSpec(memory_space=pltpu.VMEM)
    return pl.pallas_call(
        gated_kernel,
        out_shape=[jax.ShapeDtypeStruct((rows // 2, wide // 2), jnp.bfloat16)] * 2,
        in_specs=[vmem, vmem],
        out_specs=[vmem] * 2,
        compiler_params=pltpu.CompilerParams(vmem_limit_bytes=16 << 20),
        cost_estimate=pl.CostEstimate(flops=8 * rows * wide, bytes_accessed=4 << 20, transcendentals=rows * wide // 2),
    )(kept, received)


def gather_kernel(place, *refs):
    blocks, out = refs[:4], refs[4]
    for zh in range(2):
        for q in range(2):

            @pl.when((place[1] == zh) & (place[6] == q))
            def _(zh=zh, q=q):
                for other in range(2):
                    base = (zh ^ other) * 896
                    low, high = blocks[2 * q + other], blocks[2 * (1 - q) + other]
                    out[:, base : base + 384] = low[:, :384]
                    out[:, base + 384 : base + 512] = jnp.concatenate([low[:, 384:], high[:, 384:]], 1)
                    out[:, base + 512 : base + 896] = high[:, :384]


def gather(place, blocks):
    vmem = pl.BlockSpec(memory_space=pltpu.VMEM)
    return pl.pallas_call(
        gather_kernel,
        out_shape=jax.ShapeDtypeStruct((blocks[0].shape[0], 1792), jnp.bfloat16),
        in_specs=[pl.BlockSpec(memory_space=pltpu.SMEM)] + [vmem] * 4,
        out_specs=vmem,
        compiler_params=pltpu.CompilerParams(vmem_limit_bytes=16 << 20),
        cost_estimate=pl.CostEstimate(flops=0, bytes_accessed=2 << 20, transcendentals=0),
    )(place, *blocks)


def along_y(value, d):
    return move(value, lambda x, y, z, c: (x, y - d - 2 * c, z, c))


def after(value, *others):
    return lax.optimization_barrier((value, *others))[0]


def per_device(tokens, gate_weight, up_weight):
    y, zh, x, zl, c = (lax.axis_index(a) for a in AXES)
    ahead = side(x, c)
    partner, summer = (x + ahead + 4) % 4, (x - ahead + 4) % 4
    over = (summer - ahead + 4) % 4
    q = ((x + 1 - c) // 2) % 2
    rows = tokens.shape[0] // NX

    def places(a, b):
        return jnp.stack([y, zh, zl, c, a, b, q]).astype(jnp.int32)

    send_place, keep_place = places(summer, over), places(x, partner)

    panel = lax.all_gather(tokens, ("zh", "zl", "c"), axis=0)
    near, away, give_near, give_away = cut(keep_place, gate_weight, up_weight)
    got_near, got_away = move(give_near, to_partner), move(give_away, to_partner)
    near = jnp.stack([near, got_near])
    near = [near, along_y(near, 1), near, along_y(near, 3)]

    panel = after(panel, got_away, near[1], near[3])
    away, got_away, near[2], panel = lax.optimization_barrier((away, got_away, near[1], panel))
    own, shared = (p.reshape(2, 8, NX, rows, 256) for p in (panel, move(panel, to_partner)))
    far = [move(away, to_antipode)]
    near[2] = along_y(near[2], 1)
    far.append(move(after(got_away, far[0]), to_antipode))
    one, three = along_y(far[0], 1), along_y(far[0], 3)
    far[0] = [far[0], one, along_y(one, 1), three]
    sent = product(0, (0, 1), send_place, own, near, far)
    block = after(far[1], *far[0][1:])
    one, three = along_y(block, 1), along_y(block, 3)
    far[1] = [block, one, along_y(after(one, sent[0]), 1), three]

    kept = product(0, (0, 1), after(keep_place, *sent), own, near, far)
    sums, turn = [None, None], after(send_place, kept[0])
    for half in (1, 0):
        total = product(1, (half,), turn, shared, near, far, sent[half : half + 1])[0]
        turn, sums[half] = after(send_place, total), move(total, to_summer)
    total = product(1, (1,), after(keep_place, total), shared, near, far, kept[1:])[0]
    over_z, over_both = gated(total, sums[1])
    total = product(1, (0,), after(keep_place, over_z), shared, near, far, kept[:1])[0]
    over_z, over_both = move(over_z, to_antipode), move(over_both, to_both)
    mine, over_x = gated(total, after(sums[0], over_z, over_both))
    blocks = [mine, over_z, move(over_x, to_partner), over_both]
    return gather(keep_place, blocks)


def solution(mesh):
    fine = Mesh(np.array(mesh.devices).reshape(NY, 2, NX, NZ // 2, NC), AXES)
    rows, cols = ("y", "zh"), ("zl", "c")
    return jax.shard_map(
        per_device,
        mesh=fine,
        in_specs=(P(rows, ("x", *cols)), P(("x", *rows), cols), P(("x", *rows), cols)),
        out_specs=P((*rows, "x"), cols),
        check_vma=False,
    )
```

```python
import functools

import jax
import jax.numpy as jnp
import numpy as np
from jax import lax
from jax.experimental import pallas as pl
from jax.experimental.pallas import tpu as pltpu
from jax.sharding import Mesh
from jax.sharding import PartitionSpec as P

NX, NY, NZ, NC = 4, 4, 8, 2
AXES = ("y", "zh", "x", "zl", "c")
TILE = 128


def device_index(x, y, z, c):
    return ((y * 2 + z // 4) * NX + x) * 8 + (z % 4) * 2 + c


def side(x, c):
    return 1 - 2 * ((x + c) % 2)


def move(value, target):
    pairs = []
    for x in range(NX):
        for y in range(NY):
            for z in range(NZ):
                for c in range(NC):
                    tx, ty, tz, tc = target(x, y, z, c)
                    pairs.append((device_index(x, y, z, c), device_index(tx % NX, ty % NY, tz % NZ, tc)))
    return lax.ppermute(value, AXES, pairs)


def to_partner(x, y, z, c):
    return x + side(x, c), y, z, c


def to_crossed(x, y, z, c):
    return x + side(x, 1 - c), y, z, 1 - c


def to_antipode(x, y, z, c):
    return x, y, z + 4, c


def to_both(x, y, z, c):
    return x + side(x, c), y, z + 4, c


def to_summer(x, y, z, c):
    return x - side(x, c), y, z, c


def product_kernel(u, halves, place, panel, *refs):
    near, far, refs = refs[:4], refs[4:8], refs[8:]
    n = len(halves)
    before, outs, (pieces, lhs, rhs, lhs_sem, rhs_sem) = refs[: u * n], refs[u * n : u * n + n], refs[u * n + n :]
    y, zh = place[0], place[1]
    rows, wide = pieces.shape[3], rhs.shape[1]
    tokens = []
    for i, half in enumerate(halves):
        for j in range(2):
            source = panel.at[lax.rem(zh + half, 2), :, place[4 + j]]
            tokens.append(pltpu.make_async_copy(source, pieces.at[i, j], lhs_sem.at[2 * i + j]))
    weights = []
    for d in range(4):
        k = lax.rem(y + d + d % 2 * 2 * place[3], 4) * 2
        for source, at in ((near[d].at[u], k + zh), (far[d], k + 1 - zh)):
            target = rhs.at[pl.ds(pl.multiple_of(at * 256, 256), 256)]
            weights.append(pltpu.make_async_copy(source, target, rhs_sem.at[len(weights)]))
    for copy in (*tokens, *weights):
        copy.start()
    for i in range(n):
        for j in range(2):
            tokens[2 * i + j].wait()
            at = (i * 2 + j) * rows
            for k in range(8):
                lhs[at : at + rows, k * 256 : (k + 1) * 256] = pieces[i, j, k]
    for copy in weights:
        copy.wait()
    for lo in range(0, wide, 256):
        hi = min(lo + 256, wide)
        part = jnp.dot(lhs[...], rhs[:, lo:hi], preferred_element_type=jnp.float32)
        for i, out in enumerate(outs):
            mine = part[i * 2 * rows : (i + 1) * 2 * rows]
            out[:, lo:hi] = before[i][:, lo:hi] + mine if u else mine


def product(u, halves, place, panel, near, far, before=()):
    rows, depth, wide, n = panel.shape[3], 2048, far[u][0].shape[1], len(halves)
    hbm, vmem = pl.BlockSpec(memory_space=pltpu.HBM), pl.BlockSpec(memory_space=pltpu.VMEM)
    operands = [panel, *near, *far[u]]
    return pl.pallas_call(
        functools.partial(product_kernel, u, halves),
        out_shape=[jax.ShapeDtypeStruct((2 * rows, wide), jnp.float32)] * n,
        in_specs=[pl.BlockSpec(memory_space=pltpu.SMEM)] + [hbm] * len(operands) + [vmem] * len(before),
        out_specs=[vmem] * n,
        scratch_shapes=[
            pltpu.VMEM((n, 2, 8, rows, 256), jnp.bfloat16),
            pltpu.VMEM((2 * n * rows, depth), jnp.bfloat16),
            pltpu.VMEM((depth, wide), jnp.bfloat16),
            pltpu.SemaphoreType.DMA((2 * n,)),
            pltpu.SemaphoreType.DMA((8,)),
        ],
        compiler_params=pltpu.CompilerParams(vmem_limit_bytes=(40 if u else 60) << 20),
        cost_estimate=pl.CostEstimate(flops=4 * n * rows * depth * wide, bytes_accessed=8 * n << 20, transcendentals=0),
    )(place, *operands, *before)


def cut_kernel(place, gate, up, near, away, give_near, give_away):
    for zh in range(2):
        for q in range(2):

            @pl.when((place[1] == zh) & (place[6] == q))
            def _(zh=zh, q=q):
                for out, half, side_q in ((near, zh, q), (away, 1 - zh, q), (give_near, zh, 1 - q), (give_away, 1 - zh, 1 - q)):
                    base = half * 896
                    for t in range(3):
                        lo = base + side_q * 512 + t * TILE
                        out[:, 2 * t * TILE : (2 * t + 1) * TILE] = gate[:, lo : lo + TILE]
                        out[:, (2 * t + 1) * TILE : (2 * t + 2) * TILE] = up[:, lo : lo + TILE]
                    lo = base + 384 + side_q * 64
                    out[:, 6 * TILE :] = jnp.concatenate([gate[:, lo : lo + 64], up[:, lo : lo + 64]], 1)


def cut(place, gate, up):
    vmem = pl.BlockSpec(memory_space=pltpu.VMEM)
    depth, wide = gate.shape[0], gate.shape[1] // 2
    return pl.pallas_call(
        cut_kernel,
        out_shape=[jax.ShapeDtypeStruct((depth, wide), gate.dtype)] * 4,
        in_specs=[pl.BlockSpec(memory_space=pltpu.SMEM), vmem, vmem],
        out_specs=[vmem] * 4,
        compiler_params=pltpu.CompilerParams(vmem_limit_bytes=24 << 20),
        cost_estimate=pl.CostEstimate(flops=0, bytes_accessed=4 << 20, transcendentals=0),
    )(place, gate, up)


def gated_kernel(kept, received, *outs):
    rows, whole = outs[0].shape[0], kept.shape[1] // (2 * TILE)
    for n, out in enumerate(outs):
        at = slice(n * rows, (n + 1) * rows)
        total = kept[at, :] + received[at, :]
        for t in range(whole):
            gate, up = total[:, 2 * t * TILE : (2 * t + 1) * TILE], total[:, (2 * t + 1) * TILE : (2 * t + 2) * TILE]
            out[:, t * TILE : (t + 1) * TILE] = (jax.nn.silu(gate) * up).astype(jnp.bfloat16)
        last = total[:, 2 * whole * TILE :]
        up = pltpu.roll(last, TILE // 2, 1)
        out[:, whole * TILE :] = (jax.nn.silu(last) * up).astype(jnp.bfloat16)[:, : TILE // 2]


def gated(kept, received):
    rows, wide = kept.shape
    vmem = pl.BlockSpec(memory_space=pltpu.VMEM)
    return pl.pallas_call(
        gated_kernel,
        out_shape=[jax.ShapeDtypeStruct((rows // 2, wide // 2), jnp.bfloat16)] * 2,
        in_specs=[vmem, vmem],
        out_specs=[vmem] * 2,
        compiler_params=pltpu.CompilerParams(vmem_limit_bytes=16 << 20),
        cost_estimate=pl.CostEstimate(flops=8 * rows * wide, bytes_accessed=4 << 20, transcendentals=rows * wide // 2),
    )(kept, received)


def gather_kernel(place, *refs):
    blocks, out = refs[:4], refs[4]
    for zh in range(2):
        for q in range(2):

            @pl.when((place[1] == zh) & (place[6] == q))
            def _(zh=zh, q=q):
                for other in range(2):
                    base = (zh ^ other) * 896
                    low, high = blocks[2 * q + other], blocks[2 * (1 - q) + other]
                    out[:, base : base + 384] = low[:, :384]
                    out[:, base + 384 : base + 512] = jnp.concatenate([low[:, 384:], high[:, 384:]], 1)
                    out[:, base + 512 : base + 896] = high[:, :384]


def gather(place, blocks):
    vmem = pl.BlockSpec(memory_space=pltpu.VMEM)
    return pl.pallas_call(
        gather_kernel,
        out_shape=jax.ShapeDtypeStruct((blocks[0].shape[0], 1792), jnp.bfloat16),
        in_specs=[pl.BlockSpec(memory_space=pltpu.SMEM)] + [vmem] * 4,
        out_specs=vmem,
        compiler_params=pltpu.CompilerParams(vmem_limit_bytes=16 << 20),
        cost_estimate=pl.CostEstimate(flops=0, bytes_accessed=2 << 20, transcendentals=0),
    )(place, *blocks)


def along_y(value, d):
    return move(value, lambda x, y, z, c: (x, y - d - 2 * c, z, c))


def after(value, *others):
    return lax.optimization_barrier((value, *others))[0]


def per_device(tokens, gate_weight, up_weight):
    y, zh, x, zl, c = (lax.axis_index(a) for a in AXES)
    ahead = side(x, c)
    partner, summer = (x + ahead + 4) % 4, (x - ahead + 4) % 4
    over = (summer - ahead + 4) % 4
    q = ((x + 1 - c) // 2) % 2
    rows = tokens.shape[0] // NX

    def places(a, b):
        return jnp.stack([y, zh, zl, c, a, b, q]).astype(jnp.int32)

    send_place, keep_place = places(summer, over), places(x, partner)

    panel = lax.all_gather(tokens, ("zh", "zl", "c"), axis=0)
    near, away, give_near, give_away = cut(keep_place, gate_weight, up_weight)
    got_near, got_away = move(give_near, to_partner), move(give_away, to_partner)
    near = jnp.stack([near, got_near])
    near = [near, along_y(near, 1), near, along_y(near, 3)]

    panel = after(panel, got_away, near[1], near[3])
    away, got_away, near[2], panel = lax.optimization_barrier((away, got_away, near[1], panel))
    own, shared = (p.reshape(2, 8, NX, rows, 256) for p in (panel, move(panel, to_partner)))
    far = [move(away, to_antipode)]
    near[2] = along_y(near[2], 1)
    far.append(move(after(got_away, far[0]), to_antipode))
    one, three = along_y(far[0], 1), along_y(far[0], 3)
    far[0] = [far[0], one, along_y(one, 1), three]
    sent = product(0, (0, 1), send_place, own, near, far)
    block = after(far[1], *far[0][1:])
    one, three = along_y(block, 1), along_y(block, 3)
    far[1] = [block, one, along_y(after(one, sent[0]), 1), three]

    kept = product(0, (0, 1), after(keep_place, *sent), own, near, far)
    sums, turn = [None, None], after(send_place, kept[0])
    for half in (1, 0):
        total = product(1, (half,), turn, shared, near, far, sent[half : half + 1])[0]
        turn, sums[half] = after(send_place, total), move(total, to_summer)
    total = product(1, (1,), after(keep_place, total), shared, near, far, kept[1:])[0]
    over_z, over_both = gated(total, sums[1])
    total = product(1, (0,), after(keep_place, over_z), shared, near, far, kept[:1])[0]
    over_z, over_both = move(over_z, to_antipode), move(over_both, to_both)
    mine, over_x = gated(total, after(sums[0], over_z, over_both))
    blocks = [mine, over_z, move(over_x, to_partner), over_both]
    return gather(keep_place, blocks)


def solution(mesh):
    fine = Mesh(np.array(mesh.devices).reshape(NY, 2, NX, NZ // 2, NC), AXES)
    rows, cols = ("y", "zh"), ("zl", "c")
    return jax.shard_map(
        per_device,
        mesh=fine,
        in_specs=(P(rows, ("x", *cols)), P(("x", *rows), cols), P(("x", *rows), cols)),
        out_specs=P((*rows, "x"), cols),
        check_vma=False,
    )
```
